256 devices in a mesh: gx: 32 (over z, y), gy: 4 (over x_hi, core), role: 2 (over x_lo).
Axes of the slice: x: 4 (x_hi: 2, x_lo: 2; x = x_hi * 2 + x_lo), y: 4, z: 8, core: 2. Of those that a mesh axis runs over, the one named last changes fastest.
Arguments:
- velocity: float32 [3, 512, 64, 256], P(None, 'gx', 'gy', 'role'), may hold values from -6 to 6
- target_visc: bfloat16 [256, 32, 128], P('gx', 'gy', 'role'), may hold values from 0.049804688 to 1
- w_first: bfloat16 [64, 81], replicated, may hold values from -2 to 2
- w_hidden: bfloat16 [64, 1728], replicated, may hold values from -0.3125 to 0.3125
- w_last: bfloat16 [64], replicated, may hold values from -1.5 to 1.5
- sample_owner: int32 [4, 2, 256, 1], P('gy', 'role'), may hold values from 0 to 31; in each aligned block of 8 rows (0 to 7, 8 to 15, ..., all dimensions but the last counted through in order) at most 2 rows name the same one
- sample_block: int32 [4, 2, 256, 1], P('gy', 'role'), may hold values from 0 to 7
Outputs:
- u_next: float32 [3, 512, 64, 256], P(None, 'gx', 'gy', 'role')
- slot_loss: float32 [4, 2, 256], P('gy', 'role', 'gx')
- grad_first: float32 [64, 81], replicated
- grad_hidden: float32 [64, 1728], replicated
- grad_last: float32 [64], replicated
The draws below stay inside these ranges and needn't reach their ends.
Inputs may be any that keep to these rules, and one draw needn't show every extreme that they name: `sample_owner`: within one trainer's 8 rows (aligned blocks of rows) no gx index is named more than 2 times.
All inputs are finite; a program needn't handle non-finite values.
Results may differ from the reference program's by a relative error of at most 0.002.
The reference program's roundings to bfloat16 on the way (of `filtered`, `act_first`, `act_hidden`, `d_logit`, `d_hidden` and `d_first`) count: a program that leaves them out, or rounds other values in their place, can miss the bound.
Values may be sent and summed in bfloat16 or wider, within the bound.
A program may use at most 128 MiB of HBM per device.

```python
import math
import jax
import jax.numpy as jnp
import numpy as np
from jax import lax

CX = 16
CY = 16
CZ = 128
BSIDE = 8
CH = 64
SLOTS = 8
NX = 512
NY = 64
NZ = 256
NXC = 256
NYC = 32
NZC = 128
BLK = 8
CAP = 2
TRAINERS = 256
YSLABS = 4
ZSLABS = 2
LISTLEN = 256
N_GX = 32
N_GY = 4
N_ROLE = 2


def plant(array, stream_key, smallest, top_value):
    dims = array.shape
    index_at = [jax.random.randint(jax.random.fold_in(stream_key, axis), (), 0, dims[axis]) for axis in range(len(dims))]
    array = array.at[tuple(index_at)].set(smallest)
    longest = dims.index(max(dims))
    index_at[longest] = (index_at[longest] + 1) % dims[longest]
    return array.at[tuple(index_at)].set(top_value)


def shard_levels(rng, shape, shards, least, largest):
    gain = 1.0
    for axis_at, shards_of in shards:
        draws = jax.random.uniform(jax.random.fold_in(jax.random.fold_in(rng, 6), axis_at), (shards_of,), jnp.float32, least / len(shards), largest / len(shards))
        gain = gain * jnp.repeat(jnp.exp(draws), shape[axis_at] // shards_of).reshape((-1,) + (1,) * (len(shape) - 1 - axis_at))
    return gain


def routed_block(stream_key, own, number, rows, amount, top, most, lean):
    order = jax.random.permutation(stream_key, amount)
    packed, ordinary = shares(amount, rows * top, most, lean, True), shares(amount, rows * top, most, lean, False)
    places = jnp.arange(amount)

    def named(lengths, offset_by):
        used = int((lengths > 0).sum())
        fixed = max(1, used // 4)
        moved = fixed + (places - fixed + offset_by * (used - fixed)) % max(1, amount - fixed)
        return jnp.zeros((amount,), jnp.int32).at[order[jnp.where(places < fixed, places, moved)]].set(jnp.asarray(lengths, jnp.int32))

    lengths = jnp.where(number % 4 == 0, named(packed, number // 4), named(ordinary, number - number // 4 - 1))
    mixed = jax.random.permutation(jax.random.fold_in(own, 3), amount)
    donor, sink = mixed[0:amount // 2 * 2:2], mixed[1:amount // 2 * 2:2]
    margin = jnp.minimum(lengths[donor] - 1, most - lengths[sink]) // 2
    margin = jnp.where((donor == order[0]) | (sink == order[0]) | (lengths[sink] == 0), 0, jnp.maximum(margin, 0))
    moved = jax.random.randint(jax.random.fold_in(own, 4), (amount // 2,), 0, 1 << 20) % (margin + 1)
    lengths = lengths.at[donor].add(-moved).at[sink].add(moved)
    labels = jnp.searchsorted(jnp.cumsum(lengths), jnp.arange(rows * top), side="right").astype(jnp.int32)
    grid = labels.reshape(top, rows).T
    grid = grid[jax.random.permutation(jax.random.fold_in(own, 1), rows)]
    offset_by = jax.random.randint(jax.random.fold_in(own, 2), (rows, 1), 0, top)
    return jnp.take_along_axis(grid, (jnp.arange(top)[None, :] + offset_by) % top, axis=1)


def shares(number_of, total, most, lean, full):
    loads = [(1 << 20) // math.isqrt(rank ** lean) + 1 for rank in range(1, number_of + 1)]
    largest = most if full else min(most, max(-(-total // number_of), total * loads[0] // sum(loads)))
    least = 1 if total - largest >= number_of - 1 else 0
    given, spare = [largest] + [least] * (number_of - 1), total - largest - least * (number_of - 1)
    while spare > 0:
        candidates = [i for i in range(1, number_of) if given[i] < largest] or [i for i in range(1, number_of) if given[i] < most]
        mass, remaining = sum([loads[i] for i in candidates]), spare
        for i in candidates:
            extra = min(most - given[i], max(1, remaining * loads[i] // mass), spare)
            given[i] = given[i] + extra
            spare = spare - extra
    return np.array(given)


def normal_values(key, extent, scale, most, pieces=(), held_as=jnp.bfloat16):
    values = jax.random.normal(key, extent, jnp.float32) * scale
    if len(pieces) > 0:
        values = shard_levels(key, extent, pieces, -0.22, 0.18) * values
    return jnp.clip(values, min=-most, max=most).astype(held_as)


def setup_inputs(seed: int = 0) -> dict:
    seeds = jax.random.split(jax.random.key(seed), 8)
    velocity = normal_values(seeds[0], (3, NX, NY, NZ), 1.0, 6.0, ((1, 32), (2, 4), (3, 2)), jnp.float32)
    target_visc = jnp.clip(jnp.exp(math.log(1.0) - 2.9996462 * jax.random.uniform(seeds[1], (NXC, NYC, NZC), jnp.float32) ** shard_levels(seeds[1], (NXC, NYC, NZC), ((0, 32), (1, 4), (2, 2)), -0.2, 0.2)), 0.049804688, 1.0).astype(jnp.bfloat16)
    w_first = normal_values(seeds[2], (CH, 81), 9 ** -0.5, 2.0)
    w_hidden = normal_values(seeds[3], (CH, 27 * CH), (27 * CH // 4) ** -0.5, 0.3125)
    w_last = normal_values(seeds[4], (CH,), (CH // 4) ** -0.5, 1.5)
    sample_owner_keys = jax.random.split(jax.random.fold_in(seeds[5], 1), YSLABS * ZSLABS * LISTLEN // SLOTS)
    sample_owner_turns = jax.random.permutation(jax.random.fold_in(seeds[5], 3), YSLABS * ZSLABS * LISTLEN // SLOTS)
    sample_owner = jax.vmap(lambda own, number: routed_block(jax.random.fold_in(seeds[5], 2), own, number, SLOTS, N_GX, 1, CAP, 2))(sample_owner_keys, sample_owner_turns).reshape((YSLABS, ZSLABS, LISTLEN, 1))
    sample_block = plant(jax.random.randint(seeds[6], (YSLABS, ZSLABS, LISTLEN, 1), 0, BLK), jax.random.fold_in(seeds[6], 1), 0, BLK - 1).astype(jnp.int32)
    return {"velocity": velocity, "target_visc": target_visc, "w_first": w_first, "w_hidden": w_hidden, "w_last": w_last, "sample_owner": sample_owner, "sample_block": sample_block}


base_visc = 0.02
time_step = 0.2


def cell_masks(side):
    count = side ** 3
    flat = jnp.arange(count, dtype=jnp.int32)
    first = flat // (side * side)
    second = (flat // side) % side
    third = flat % side
    rows = []
    for k in range(27):
        shift_x = k // 9 - 1
        shift_y = (k // 3) % 3 - 1
        shift_z = k % 3 - 1
        inside = (first + shift_x >= 0) & (first + shift_x < side)
        inside = inside & (second + shift_y >= 0) & (second + shift_y < side)
        inside = inside & (third + shift_z >= 0) & (third + shift_z < side)
        rows.append(inside)
    return jnp.stack(rows).astype(jnp.float32)


def pad_cells(field, side):
    reach = side * side + side + 1
    return jnp.pad(field, ((0, 0), (0, 0), (reach, reach)))


def shifted(padded, masks, side, k, count):
    reach = side * side + side + 1
    offset = (k // 9 - 1) * side * side + ((k // 3) % 3 - 1) * side + (k % 3 - 1)
    return lax.slice_in_dim(padded, reach + offset, reach + offset + count, axis=2) * masks[k]


def convolve(weight, field, masks, side):
    inner = field.shape[1]
    count = field.shape[2]
    padded = pad_cells(field.astype(jnp.float32), side)
    wide = weight.astype(jnp.float32)
    summed = None
    for k in range(27):
        term = jnp.einsum("oc,bcn->bon", wide[:, k * inner:(k + 1) * inner], shifted(padded, masks, side, k, count))
        summed = term if summed is None else summed + term
    return summed


def silu_slope(value):
    sig = jax.nn.sigmoid(value)
    return sig * (1.0 + value * (1.0 - sig))


def network(w_first, w_hidden, w_last, inputs, masks, side):
    pre_first = convolve(w_first, inputs, masks, side)
    act_first = jax.nn.silu(pre_first).astype(jnp.bfloat16)
    pre_hidden = convolve(w_hidden, act_first, masks, side)
    act_hidden = jax.nn.silu(pre_hidden).astype(jnp.bfloat16)
    logits = jnp.einsum("c,bcn->bn", w_last.astype(jnp.float32), act_hidden.astype(jnp.float32))
    eddy = 0.5 * jax.nn.softplus(logits)
    return pre_first, act_first, pre_hidden, act_hidden, logits, eddy


def fit_blocks(w_first, w_hidden, w_last, blocks, masks, side):
    count = blocks.shape[2]
    width = w_hidden.shape[0]
    inputs = blocks[:, :3]
    target = blocks[:, 3].astype(jnp.float32)
    pre_first, act_first, pre_hidden, act_hidden, logits, eddy = network(w_first, w_hidden, w_last, inputs, masks, side)
    error = eddy - target
    losses = jnp.mean(error * error, axis=1)
    d_logit = (error * jax.nn.sigmoid(logits) / (TRAINERS * count)).astype(jnp.bfloat16)
    grad_last = jnp.einsum("bn,bcn->c", d_logit.astype(jnp.float32), act_hidden.astype(jnp.float32))
    d_hidden = (w_last.astype(jnp.float32)[None, :, None] * d_logit.astype(jnp.float32)[:, None, :] * silu_slope(pre_hidden)).astype(jnp.bfloat16)
    wide_delta = d_hidden.astype(jnp.float32)
    padded_act = pad_cells(act_first.astype(jnp.float32), side)
    grad_hidden = jnp.concatenate([jnp.einsum("bon,bcn->oc", wide_delta, shifted(padded_act, masks, side, k, count)) for k in range(27)], axis=1)
    padded_delta = pad_cells(wide_delta, side)
    wide_hidden = w_hidden.astype(jnp.float32)
    d_act = None
    for k in range(27):
        term = jnp.einsum("oc,bon->bcn", wide_hidden[:, k * width:(k + 1) * width], shifted(padded_delta, masks, side, 26 - k, count))
        d_act = term if d_act is None else d_act + term
    d_first = (d_act * silu_slope(pre_first)).astype(jnp.bfloat16)
    wide_first = d_first.astype(jnp.float32)
    padded_in = pad_cells(inputs.astype(jnp.float32), side)
    grad_first = jnp.concatenate([jnp.einsum("bon,bcn->oc", wide_first, shifted(padded_in, masks, side, k, count)) for k in range(27)], axis=1)
    return losses, grad_first, grad_hidden, grad_last


def reference(velocity, target_visc, w_first, w_hidden, w_last, sample_owner, sample_block):
    side = BSIDE
    count = side ** 3
    masks = cell_masks(side)
    filtered = velocity.reshape(3, NXC, 2, NYC, 2, NZC, 2).mean(axis=(2, 4, 6)).astype(jnp.bfloat16)
    count_x = NXC // side
    count_y = NYC // side
    count_z = NZC // side
    joined = jnp.concatenate([filtered, target_visc[None]], axis=0)
    blocks = joined.reshape(4, count_x, side, count_y, side, count_z, side).transpose(1, 3, 5, 0, 2, 4, 6)
    blocks = blocks.reshape(count_x, count_y, count_z, 4, count)

    def infer_row(row_blocks):
        return network(w_first, w_hidden, w_last, row_blocks[:, :3], masks, side)[5]

    eddy_rows = lax.map(infer_row, blocks.reshape(count_x, count_y * count_z, 4, count))
    eddy_field = eddy_rows.reshape(count_x, count_y, count_z, side, side, side).transpose(0, 3, 1, 4, 2, 5).reshape(NXC, NYC, NZC)
    visc = base_visc + jnp.repeat(jnp.repeat(jnp.repeat(eddy_field, 2, 0), 2, 1), 2, 2)

    advect = jnp.zeros_like(velocity)
    diffuse = jnp.zeros_like(velocity)
    for axis in range(3):
        dim = axis + 1
        ahead_one = jnp.roll(velocity, -1, dim)
        behind_one = jnp.roll(velocity, 1, dim)
        ahead_two = jnp.roll(velocity, -2, dim)
        behind_two = jnp.roll(velocity, 2, dim)
        slope = (8.0 * (ahead_one - behind_one) - (ahead_two - behind_two)) / 12.0
        advect = advect + velocity[axis][None] * slope
        visc_ahead = 0.5 * (visc + jnp.roll(visc, -1, axis))
        visc_behind = 0.5 * (visc + jnp.roll(visc, 1, axis))
        diffuse = diffuse + visc_ahead[None] * (ahead_one - velocity) - visc_behind[None] * (velocity - behind_one)
    u_next = velocity + time_step * (diffuse - advect)

    per_x = CX // (2 * side)
    per_y = CY // (2 * side)
    per_z = CZ // (2 * side)
    owners = sample_owner[..., 0].reshape(N_GY, N_ROLE, N_GX, SLOTS)
    picks = sample_block[..., 0].reshape(N_GY, N_ROLE, N_GX, SLOTS)
    local_x = picks // (per_y * per_z)
    local_y = (picks // per_z) % per_y
    local_z = picks % per_z
    block_x = owners * per_x + local_x
    block_y = jnp.arange(N_GY, dtype=jnp.int32)[:, None, None, None] * per_y + local_y
    block_z = jnp.arange(N_ROLE, dtype=jnp.int32)[None, :, None, None] * per_z + local_z
    index_x = block_x.reshape(TRAINERS, SLOTS)
    index_y = block_y.reshape(TRAINERS, SLOTS)
    index_z = block_z.reshape(TRAINERS, SLOTS)

    def train_step(carry, indices):
        picked = blocks[indices[0], indices[1], indices[2]]
        losses, grad_first, grad_hidden, grad_last = fit_blocks(w_first, w_hidden, w_last, picked, masks, side)
        return (carry[0] + grad_first, carry[1] + grad_hidden, carry[2] + grad_last), losses

    start = (jnp.zeros(w_first.shape, jnp.float32), jnp.zeros(w_hidden.shape, jnp.float32), jnp.zeros(w_last.shape, jnp.float32))
    grads, losses = lax.scan(train_step, start, (index_x, index_y, index_z))
    slot_loss = losses.reshape(N_GY, N_ROLE, N_GX * SLOTS)
    return u_next, slot_loss, grads[0], grads[1], grads[2]
```

```python
import numpy as np
import jax
import jax.numpy as jnp
from jax import lax
from jax.sharding import PartitionSpec as P
from jax.experimental import pallas as pl
from jax.experimental.pallas import tpu as pltpu

SIDE = 8
CH = 64
F32 = jnp.float32
BF16 = jnp.bfloat16
NT = (((1,), (1,)), ((), ()))
NN = (((1,), (0,)), ((), ()))


def dot(a, b, dims=NN):
    return lax.dot_general(a, b, dims, preferred_element_type=F32)


def pool_matrix():
    z = np.arange(128)[:, None]
    lane = np.arange(256)[None, :]
    block, inner = lane // 32, lane % 32
    parts = []
    for comp in range(3):
        hit = (inner < 24) & (inner % 3 == comp) & (z // 2 == block * 8 + inner // 3)
        parts.append(np.where(hit, 0.125, 0.0))
    return np.concatenate(parts, 0).astype(jnp.bfloat16)


def target_matrix():
    z = np.arange(64)[:, None]
    lane = np.arange(256)[None, :]
    block, inner = lane // 32, lane % 32
    return ((inner >= 24) & (z == block * 8 + inner - 24)).astype(jnp.bfloat16)


def spread_matrix():
    row = np.arange(128)[:, None]
    lane = np.arange(512)[None, :]
    return (row == 24 + lane // 64).astype(jnp.bfloat16)


def first_selector():
    out = np.zeros((81, 3, 8, 128), np.float32)
    for i in range(3):
        for zo in range(8):
            for j in range(3):
                for t in range(9):
                    zi = zo - 1 + t // 3
                    if 0 <= zi < 8:
                        out[9 * (3 * i + j) + t, i, zo, j * 32 + zi * 3 + t % 3] = 1.0
    return out.reshape(81, 3072).astype(jnp.bfloat16)


def lane_of(shape):
    return lax.broadcasted_iota(jnp.int32, shape, len(shape) - 1)


def shift_y(field, shift):
    zero = jnp.zeros((8, 8, field.shape[2]), field.dtype)
    if shift < 0:
        return jnp.concatenate([zero, field[:, :56]], axis=1)
    if shift > 0:
        return jnp.concatenate([field[:, 8:], zero], axis=1)
    return field


def widen(store, field):
    lane = lane_of((512, 128))
    zero = jnp.zeros((64, 1152), BF16)
    near = [
        jnp.where(lane >= 64, pltpu.roll(field[:, 256:384], 64, 1), 0.0),
        jnp.where(lane < 64, pltpu.roll(field[:, 128:256], 64, 1), 0.0),
    ]
    for half in range(2):
        store[half, 0] = zero
        store[half, 9] = zero
        whole = jnp.concatenate([field[:, half * 256 : half * 256 + 256], near[half]], axis=1)
        whole = whole.reshape(8, 64, 384)
        for j in range(3):
            store[half, 1:9, :, j * 384 : (j + 1) * 384] = shift_y(whole, j - 1).astype(BF16)


def rows_of(store, half, i):
    return store[half, i : i + 8].reshape(512, 1152)


def place_weights(w_hidden, ahead, back):
    lane = lane_of((64, 128))
    low = lane < 64
    zero = jnp.zeros((64, 128), BF16)
    tiles = [w_hidden[:, t * 128 : (t + 1) * 128] for t in range(13)]
    last = w_hidden[:, 1664:1728]
    tiles.append(jnp.concatenate([last, last], axis=1))
    tiles = [t.astype(F32) for t in tiles]
    swapped = [pltpu.roll(t, 64, 1) for t in tiles]
    for j in range(9):
        t = 3 * j // 2
        if j % 2 == 0:
            ab = tiles[t]
            bc = jnp.where(low, swapped[t], swapped[t + 1])
            c_low, c_high = tiles[t + 1], swapped[t + 1]
            a_low, a_high = tiles[t], swapped[t]
        else:
            bc = tiles[t + 1]
            ab = jnp.where(low, swapped[t], swapped[t + 1])
            c_low, c_high = swapped[t + 1], tiles[t + 1]
            a_low, a_high = swapped[t], tiles[t]
        c_0 = jnp.where(low, c_low, 0.0).astype(BF16)
        o_c = jnp.where(low, 0.0, c_high).astype(BF16)
        a_0 = jnp.where(low, a_low, 0.0).astype(BF16)
        o_a = jnp.where(low, 0.0, a_high).astype(BF16)
        ab = ab.astype(BF16)
        bc = bc.astype(BF16)
        rows = [(bc, zero, a_0), (ab, c_0, zero), (o_a, bc, zero), (zero, ab, o_c)]
        for zo in range(4):
            for part in range(3):
                start = (j % 3) * 384 + part * 128
                ahead[j // 3, zo * 64 : (zo + 1) * 64, start : start + 128] = rows[zo][part]
        flip = 8 - j
        rows = [(bc, zero), (ab, c_0), (o_a, bc), (zero, ab), (c_0, zero), (zero, o_a)]
        for zi in range(6):
            start = (flip % 3) * 384 + zi * 64
            for part in range(2):
                back[flip // 3, start : start + 64, part * 128 : (part + 1) * 128] = rows[zi][part]


def local_kernel(
    vel, target, w_first, w_hidden, w_last, owner, block, pool, tmat, spread, sel,
    sums, visc,
    filt, first_in, w_one, ahead, back, wide_act, wide_del, slope_one, slope_two, eddy_z,
):
    place_weights(w_hidden, ahead, back)
    placed = dot(w_first[...], sel[...]).astype(BF16)
    for i in range(3):
        for zo in range(8):
            at = (i * 8 + zo) * 128
            w_one[i, zo * 64 : (zo + 1) * 64, :] = placed[:, at : at + 128]

    pooled = []
    for comp in range(3):
        total = None
        for dx in range(2):
            for dy in range(2):
                part = jnp.concatenate(
                    [vel[comp, 2 * x + dx, pl.ds(dy, 8, stride=2), :] for x in range(8)], axis=0
                )
                total = part if total is None else total + part
        pooled.append(total)
    rest = jnp.concatenate(pooled, axis=1)
    blocks = None
    for _ in range(3):
        piece = rest.astype(BF16)
        rest = rest - piece.astype(F32)
        term = dot(piece, pool[...])
        blocks = term if blocks is None else blocks + term
    blocks = blocks.astype(BF16).astype(F32)
    want = target[...].astype(F32).reshape(64, 64).astype(BF16)
    blocks = blocks + dot(want, tmat[...])
    for b in range(8):
        tile = blocks[:, (b // 4) * 128 : (b // 4) * 128 + 128]
        if b % 4:
            tile = pltpu.roll(tile, 128 - 32 * (b % 4), 1)
        filt[pl.ds(b, 64, stride=8), :] = tile
    held = filt[...]
    targets = dot(held.astype(BF16), spread[...])
    lane = lane_of((512, 128))
    inputs = jnp.where(lane < 24, held, 0.0).reshape(8, 64, 128)
    near = shift_y(inputs, -1)
    near = near + pltpu.roll(inputs.reshape(512, 128), 32, 1).reshape(8, 64, 128)
    near = near + pltpu.roll(shift_y(inputs, 1).reshape(512, 128), 64, 1).reshape(8, 64, 128)
    first_in[0] = jnp.zeros((64, 128), BF16)
    first_in[9] = jnp.zeros((64, 128), BF16)
    first_in[1:9] = near.astype(BF16)

    pre = None
    for i in range(3):
        term = dot(first_in[i : i + 8].reshape(512, 128), w_one[i], NT)
        pre = term if pre is None else pre + term
    sig = 1.0 / (1.0 + jnp.exp(-pre))
    slope_one[...] = sig * (1.0 + pre * (1.0 - sig))
    widen(wide_act, (pre * sig).astype(BF16).astype(F32))

    wl = w_last[...].astype(F32)
    wl = jnp.concatenate([wl, wl, wl, wl], axis=1)
    rows_iota = lax.broadcasted_iota(jnp.int32, (384, 256), 0)
    lanes_iota = lax.broadcasted_iota(jnp.int32, (384, 256), 1)
    cell = jnp.where(rows_iota < 256, rows_iota // 64, (rows_iota // 2) % 4)
    out_map = jnp.where(cell == lanes_iota // 64, wl, 0.0).astype(BF16)

    mine = owner[...] == lax.axis_index("gx")
    number = lax.broadcasted_iota(jnp.int32, (8, 256), 0)
    drawn = jnp.where(mine & (block[...] == number), 1.0, 0.0)
    times = jnp.sum(drawn, axis=1, keepdims=True)

    loss = jnp.zeros((8, 256), F32)
    last = jnp.zeros((8, 256), F32)
    deltas, parts = [], []
    for half in range(2):
        pre = None
        for i in range(3):
            term = dot(rows_of(wide_act, half, i), ahead[i], NT)
            pre = term if pre is None else pre + term
        sig = 1.0 / (1.0 + jnp.exp(-pre))
        act = (pre * sig).astype(BF16)
        slope = sig * (1.0 + pre * (1.0 - sig))
        both = dot(act, out_map, NT)
        logits = both[:, :256]
        eddy_z[half] = 0.5 * (
            jnp.maximum(both[:, 256:], 0.0) + jnp.log1p(jnp.exp(-jnp.abs(both[:, 256:])))
        )
        small = jnp.exp(-jnp.abs(logits))
        eddy = 0.5 * (jnp.maximum(logits, 0.0) + jnp.log1p(small))
        gate = jnp.where(logits >= 0, 1.0, small) / (1.0 + small)
        error = eddy - targets[:, half * 256 : half * 256 + 256]
        loss = loss + jnp.sum((error * error).reshape(64, 8, 256), axis=0)
        d_logit = (error * gate * (1.0 / (256 * 512))).astype(BF16).astype(F32)
        last = last + jnp.sum((d_logit * act.astype(F32)).reshape(64, 8, 256), axis=0)
        delta = (wl * d_logit * slope).astype(BF16).astype(F32)
        deltas.append(delta)
        scaled = (delta.reshape(64, 8, 256) * times.reshape(1, 8, 1)).reshape(512, 256)
        high = scaled.astype(BF16)
        low = scaled - high.astype(F32)
        parts.append(
            jnp.concatenate([scaled.T.astype(BF16), low.T.astype(BF16)], axis=0)
        )
    widen(wide_del, jnp.concatenate(deltas, axis=1))

    lane = lane_of((64, 128))
    is_low = lane < 64
    held_a = None
    for i in range(3):
        grad = None
        for half in range(2):
            term = dot(parts[half], rows_of(wide_act, half, i))
            grad = term if grad is None else grad + term
        grad = grad[:256] + grad[256:]
        for j in range(3):
            k = 3 * i + j
            g = [
                [grad[zo * 64 : zo * 64 + 64, j * 384 + p * 128 : j * 384 + p * 128 + 128] for p in range(3)]
                for zo in range(4)
            ]
            bc = g[0][0] + g[2][1]
            ab = g[1][0] + g[3][1]
            cb = pltpu.roll(bc, 64, 1)
            a_low = g[0][2] + pltpu.roll(g[2][0], 64, 1)
            ab = ab + jnp.where(is_low, a_low, cb)
            c_low = cb + g[1][1] + pltpu.roll(g[3][2], 64, 1)
            t = 3 * k // 2
            if k % 2 == 0:
                sums[t * 64 : t * 64 + 64, :] = ab
                held_a = c_low
            else:
                ba = pltpu.roll(ab, 64, 1)
                sums[t * 64 : t * 64 + 64, :] = jnp.where(is_low, held_a, ba)
                sums[(t + 1) * 64 : (t + 1) * 64 + 64, :] = jnp.where(
                    is_low, ba, pltpu.roll(c_low, 64, 1)
                )
    sums[13 * 64 : 14 * 64, :] = jnp.where(is_low, held_a, 0.0)

    firsts = []
    for half in range(2):
        d_act = None
        for i in range(3):
            term = dot(rows_of(wide_del, half, i), back[i])
            d_act = term if d_act is None else d_act + term
        d_first = (d_act * slope_one[:, half * 256 : half * 256 + 256]).astype(BF16).astype(F32)
        scaled = (d_first.reshape(64, 8, 256) * times.reshape(1, 8, 1)).reshape(512, 256)
        high = scaled.astype(BF16)
        low = scaled - high.astype(F32)
        firsts.append((scaled.T.astype(BF16), low.T.astype(BF16)))
    lhs = jnp.concatenate([firsts[0][0], firsts[1][0], firsts[0][1], firsts[1][1]], axis=0)
    packed = jnp.zeros((64, 128), F32)
    for i in range(3):
        grad = dot(lhs, first_in[i : i + 8].reshape(512, 128))
        grad = grad[:512] + grad[512:]
        total = None
        for zo in range(8):
            part = grad[zo * 64 : zo * 64 + 64]
            shift = (-3 * (zo - 1)) % 128
            part = pltpu.roll(part, shift, 1) if shift else part
            total = part if total is None else total + part
        for j in range(3):
            at = 9 * (3 * i + j)
            shift = (at - 32 * j) % 128
            moved = pltpu.roll(total, shift, 1) if shift else total
            packed = jnp.where((lane >= at) & (lane < at + 9), moved, packed)
    sums[896:960, :] = packed

    per_block = jnp.sum(loss, axis=1, keepdims=True) * (1.0 / (64 * 512))
    by_slot = jnp.sum(drawn * per_block, axis=0, keepdims=True)
    group = lax.axis_index("gy") * lax.axis_size("role") + lax.axis_index("role")
    row = lax.broadcasted_iota(jnp.int32, (16, 128), 0)
    spot = jnp.where(row % 2 == 0, by_slot[:, :128], by_slot[:, 128:])
    sums[960:976, :] = jnp.where(row // 2 == group, spot, 0.0)
    last = jnp.sum(last * times, axis=0, keepdims=True)
    last = last[:, :128] + last[:, 128:]
    last = last + pltpu.roll(last, 64, 1)
    sums[976:1024, :] = jnp.broadcast_to(last, (48, 128))

    lane = lane_of((64, 128))
    field = jnp.zeros((64, 128), F32)
    for half in range(2):
        for b in range(8):
            part = eddy_z[half, pl.ds(b, 64, stride=8), :]
            field = jnp.where(lane // 8 == 2 * b + half, part, field)
    field = 0.02 + field
    for x in range(8):
        rows = field[x * 8 : x * 8 + 8]
        for dx in range(2):
            visc[2 * x + dx, pl.ds(0, 8, stride=2), :] = rows
            visc[2 * x + dx, pl.ds(1, 8, stride=2), :] = rows


def local_part(velocity, target_visc, w_first, w_hidden, w_last, owner, block):
    consts = [jnp.asarray(a) for a in (pool_matrix(), target_matrix(), spread_matrix(), first_selector())]
    return pl.pallas_call(
        local_kernel,
        out_shape=(
            jax.ShapeDtypeStruct((1024, 128), F32),
            jax.ShapeDtypeStruct((16, 16, 128), F32),
        ),
        in_specs=[pl.BlockSpec(memory_space=pltpu.VMEM)] * 11,
        out_specs=(pl.BlockSpec(memory_space=pltpu.VMEM),) * 2,
        scratch_shapes=[
            pltpu.VMEM((512, 128), F32),
            pltpu.VMEM((10, 64, 128), BF16),
            pltpu.VMEM((3, 512, 128), BF16),
            pltpu.VMEM((3, 256, 1152), BF16),
            pltpu.VMEM((3, 1152, 256), BF16),
            pltpu.VMEM((2, 10, 64, 1152), BF16),
            pltpu.VMEM((2, 10, 64, 1152), BF16),
            pltpu.VMEM((512, 512), F32),
            pltpu.VMEM((8, 128), F32),
            pltpu.VMEM((2, 512, 128), F32),
        ],
        compiler_params=pltpu.CompilerParams(vmem_limit_bytes=48 * 1024 * 1024),
        name="local_part",
    )(
        velocity, target_visc, w_first, w_hidden, w_last.reshape(1, 64),
        owner.reshape(1, 256), block.reshape(1, 256), *consts,
    )

MESH = pl.DeviceIdType.MESH


def share_kernel(
    vel, visc, sums,
    u_next, slot_loss, grad_first, grad_hidden, grad_last,
    ext, y_out, y_in, z_out, z_in, half_in, half_sum, chunk_in, chunk_sum, deep_in, total,
    sems,
):
    gx, gy, role = lax.axis_index("gx"), lax.axis_index("gy"), lax.axis_index("role")
    depth, y = gx // 4, gx % 4
    x, core = (gy // 2) * 2 + role, gy % 2
    spot = y * 4 + x

    def plane(dy, dx):
        to_y, to_x = (y + dy) % 4, (x + dx) % 4
        return to_y * 4 + to_x, (depth * 4 + to_y, (to_x // 2) * 2 + core, to_x % 2)

    steps = [(dy, dx) for dy in range(4) for dx in range(4) if dy or dx]
    other = (gx, gy - core + 1 - core, role)
    x_up, x_down = ((gx + 1) % 32, gy, role), ((gx + 31) % 32, gy, role)
    y_up, y_down = (gx, (gy + 1) % 4, role), (gx, (gy + 3) % 4, role)
    z_side = (gx, gy, 1 - role)

    barrier = pltpu.get_barrier_semaphore()
    greeted = [plane(dy, dx)[1] for dy, dx in steps]
    greeted += [(((depth + d) % 8) * 4 + y, gy, role) for d in range(1, 8)]
    greeted += [x_up, x_down, y_up, y_down]
    for device in greeted:
        pl.semaphore_signal(barrier, inc=1, device_id=device, device_id_type=MESH)

    used = [0]

    def copy(src, dst, device):
        at = used[0]
        used[0] += 1
        return pltpu.make_async_remote_copy(
            src_ref=src, dst_ref=dst, send_sem=sems.at[0, at], recv_sem=sems.at[1, at],
            device_id=device, device_id_type=MESH,
        )

    for c in range(4):
        for h in range(1 if c == 3 else 2):
            for i in range(16):
                low = visc[i, 0:1, :] if c == 3 else vel[c, i, h : h + 1, :]
                high = visc[i, 15:16, :] if c == 3 else vel[c, i, 14 + h : 15 + h, :]
                y_out[0, 2 * c + h, i : i + 1, :] = low
                y_out[1, 2 * c + h, i : i + 1, :] = high
    lane = lane_of((16, 128))
    for c in range(4):
        for i in range(16):
            plane_of = visc[i] if c == 3 else vel[c, i]
            g = (c % 2) * 16 + i
            moved = pltpu.roll(plane_of, 2 + 4 * g, 1)
            if c % 2 == 0 and i == 0:
                packed = moved
            else:
                packed = jnp.where(lane // 4 == g, moved, packed)
            if c % 2 == 1 and i == 15:
                z_out[c // 2] = packed

    pl.semaphore_wait(barrier, len(greeted))

    first = copy(sums.at[pl.ds(pl.multiple_of((1 - core) * 512, 512), 512)], half_in, other)
    first.start()
    rims = [
        copy(vel.at[:, 0:2], ext.at[0:3, 18:20, 8:24], x_down),
        copy(vel.at[:, 14:16], ext.at[0:3, 0:2, 8:24], x_up),
        copy(visc.at[0:1], ext.at[3, 18:19, 8:24], x_down),
        copy(visc.at[15:16], ext.at[3, 1:2, 8:24], x_up),
        copy(y_out.at[0], y_in.at[1], y_down),
        copy(y_out.at[1], y_in.at[0], y_up),
        copy(z_out, z_in, z_side),
    ]
    for rim in rims:
        rim.start()
    for c in range(3):
        ext[c, 2:18, 8:24, :] = vel[c]
    ext[3, 2:18, 8:24, :] = visc[...]

    first.wait_recv()
    half_sum[...] = sums[pl.ds(pl.multiple_of(core * 512, 512), 512), :] + half_in[...]
    scatter = []
    for s, (dy, dx) in enumerate(steps):
        to, device = plane(dy, dx)
        scatter.append(
            copy(half_sum.at[pl.ds(pl.multiple_of(to * 32, 32), 32)], chunk_in.at[s], device)
        )
        scatter[-1].start()

    for rim in rims:
        rim.wait_recv()
    for c in range(4):
        for h in range(1 if c == 3 else 2):
            for i in range(16):
                at = 7 if c == 3 else 6 + h
                ext[c, 2 + i, at : at + 1, :] = y_in[0, 2 * c + h, i : i + 1, :]
                ext[c, 2 + i, 24 + h : 25 + h, :] = y_in[1, 2 * c + h, i : i + 1, :]

    def row(i, carry):
        def beside(c, here, far):
            turn = (254 - 4 * ((c % 2) * 16 + i)) % 128
            edge = pltpu.roll(z_in[c // 2], turn, 1)
            out = []
            for m in (1, 2) if far else (1,):
                after = jnp.where(lane < m, edge, here)
                before = jnp.where(lane >= 128 - m, edge, here)
                out += [pltpu.roll(after, 128 - m, 1), pltpu.roll(before, m, 1)]
            return out

        centre = ext[3, 2 + i, 8:24, :]
        sides = [
            (ext[3, 3 + i, 8:24, :], ext[3, 1 + i, 8:24, :]),
            (ext[3, 2 + i, 9:25, :], ext[3, 2 + i, 7:23, :]),
            beside(3, centre, False),
        ]
        sides = [(0.5 * (centre + a), 0.5 * (centre + b)) for a, b in sides]
        speed = [ext[c, 2 + i, 8:24, :] for c in range(3)]
        for c in range(3):
            here = speed[c]
            near = [
                [ext[c, 2 + i + m, 8:24, :] for m in (1, -1, 2, -2)],
                [ext[c, 2 + i, 8 + m : 24 + m, :] for m in (1, -1, 2, -2)],
                beside(c, here, True),
            ]
            change = None
            for axis in range(3):
                a1, b1, a2, b2 = near[axis]
                slope = (8.0 * (a1 - b1) - (a2 - b2)) * (1.0 / 12.0)
                term = sides[axis][0] * (a1 - here) - sides[axis][1] * (here - b1)
                term = term - speed[axis] * slope
                change = term if change is None else change + term
            u_next[c, i] = here + 0.2 * change
        return carry

    lax.fori_loop(0, 16, row, 0)

    for part in scatter:
        part.wait_recv()
    mine = half_sum[pl.ds(pl.multiple_of(spot * 32, 32), 32), :]
    for s in range(15):
        mine = mine + chunk_in[s]
    chunk_sum[...] = mine
    deep_in[depth] = mine
    deep = []
    for d in range(1, 8):
        device = (((depth + d) % 8) * 4 + y, gy, role)
        deep.append(copy(chunk_sum, deep_in.at[depth], device))
        deep[-1].start()
    for part in deep:
        part.wait_recv()
    mine = deep_in[0]
    for d in range(1, 8):
        mine = mine + deep_in[d]
    own = pl.ds(pl.multiple_of(core * 512 + spot * 32, 32), 32)
    total[own, :] = mine
    gather = []
    for s, (dy, dx) in enumerate(steps):
        device = plane(dy, dx)[1]
        gather.append(copy(total.at[own], total.at[own], device))
        gather[-1].start()
    across = []
    for dy in range(4):
        for part, (sy, _) in zip(gather, steps):
            if sy == dy:
                part.wait_recv()
        at = pl.ds(pl.multiple_of(core * 512 + ((y + 4 - dy) % 4) * 128, 128), 128)
        across.append(copy(total.at[at], total.at[at], other))
        across[-1].start()
    for part in across:
        part.wait_recv()

    for t in range(13):
        grad_hidden[:, t * 128 : (t + 1) * 128] = total[t * 64 : (t + 1) * 64, :]
    grad_hidden[:, 1664:1728] = total[832:896, :64]
    grad_first[...] = total[896:960, :81]
    grad_last[...] = total[976:977, :64]
    losses = total[960:976, :]
    at = lax.broadcasted_iota(jnp.int32, (16, 128), 0)
    losses = jnp.where(at == (gy * 2 + role) * 2 + gx // 16, losses, 0.0)
    losses = jnp.sum(losses, axis=0, keepdims=True)
    losses = pltpu.roll(losses, (128 - (gx % 16) * 8) % 128, 1)
    slot_loss[0] = losses[:, :8]
    for part in [first] + rims + scatter + deep + gather + across:
        part.wait_send()


COPIES = 1 + 7 + 15 + 7 + 15 + 4


def share_part(velocity, visc, sums):
    vmem = pl.BlockSpec(memory_space=pltpu.VMEM)
    return pl.pallas_call(
        share_kernel,
        out_shape=(
            jax.ShapeDtypeStruct((3, 16, 16, 128), F32),
            jax.ShapeDtypeStruct((1, 1, 8), F32),
            jax.ShapeDtypeStruct((64, 81), F32),
            jax.ShapeDtypeStruct((64, 1728), F32),
            jax.ShapeDtypeStruct((1, 64), F32),
        ),
        in_specs=[vmem] * 3,
        out_specs=(vmem,) * 5,
        scratch_shapes=[
            pltpu.VMEM((4, 20, 32, 128), F32),
            pltpu.VMEM((2, 7, 16, 128), F32),
            pltpu.VMEM((2, 7, 16, 128), F32),
            pltpu.VMEM((2, 16, 128), F32),
            pltpu.VMEM((2, 16, 128), F32),
            pltpu.VMEM((512, 128), F32),
            pltpu.VMEM((512, 128), F32),
            pltpu.VMEM((15, 32, 128), F32),
            pltpu.VMEM((32, 128), F32),
            pltpu.VMEM((8, 32, 128), F32),
            pltpu.VMEM((1024, 128), F32),
            pltpu.SemaphoreType.DMA((2, COPIES)),
        ],
        compiler_params=pltpu.CompilerParams(
            vmem_limit_bytes=48 * 1024 * 1024, collective_id=0, has_side_effects=True
        ),
        name="share_part",
    )(velocity, visc, sums)


def on_device(velocity, target_visc, w_first, w_hidden, w_last, sample_owner, sample_block):
    sums, visc = local_part(
        velocity, target_visc, w_first, w_hidden, w_last, sample_owner, sample_block
    )
    u_next, slot_loss, grad_first, grad_hidden, grad_last = share_part(velocity, visc, sums)
    return (u_next, slot_loss, grad_first, grad_hidden, grad_last.reshape(64))


def solution(mesh):
    return jax.shard_map(
        on_device,
        mesh=mesh,
        in_specs=(
            P(None, "gx", "gy", "role"),
            P("gx", "gy", "role"),
            P(),
            P(),
            P(),
            P("gy", "role", None, None),
            P("gy", "role", None, None),
        ),
        out_specs=(P(None, "gx", "gy", "role"), P("gy", "role", "gx"), P(), P(), P()),
        check_vma=False,
    )
```

```python
import numpy as np
import jax
import jax.numpy as jnp
from jax import lax
from jax.sharding import PartitionSpec as P
from jax.experimental import pallas as pl
from jax.experimental.pallas import tpu as pltpu

SIDE = 8
CH = 64
F32 = jnp.float32
BF16 = jnp.bfloat16
NT = (((1,), (1,)), ((), ()))
NN = (((1,), (0,)), ((), ()))
MESH = pl.DeviceIdType.MESH


def dot(a, b, dims=NN):
    return lax.dot_general(a, b, dims, preferred_element_type=F32)


def pool_matrix():
    z = np.arange(128)[:, None]
    lane = np.arange(256)[None, :]
    block, inner = lane // 32, lane % 32
    parts = []
    for comp in range(3):
        hit = (inner < 24) & (inner % 3 == comp) & (z // 2 == block * 8 + inner // 3)
        parts.append(np.where(hit, 0.125, 0.0))
    return np.concatenate(parts, 0).astype(jnp.bfloat16)


def target_matrix():
    z = np.arange(64)[:, None]
    lane = np.arange(256)[None, :]
    block, inner = lane // 32, lane % 32
    return ((inner >= 24) & (z == block * 8 + inner - 24)).astype(jnp.bfloat16)


def spread_matrix():
    row = np.arange(128)[:, None]
    lane = np.arange(512)[None, :]
    return (row == 24 + lane // 64).astype(jnp.bfloat16)


def first_selector():
    out = np.zeros((81, 3, 8, 128), np.float32)
    for i in range(3):
        for zo in range(8):
            for j in range(3):
                for t in range(9):
                    zi = zo - 1 + t // 3
                    if 0 <= zi < 8:
                        out[9 * (3 * i + j) + t, i, zo, j * 32 + zi * 3 + t % 3] = 1.0
    return out.reshape(81, 3072).astype(jnp.bfloat16)


def lane_of(shape):
    return lax.broadcasted_iota(jnp.int32, shape, len(shape) - 1)


def shift_y(field, shift):
    zero = jnp.zeros((8, 8, field.shape[2]), field.dtype)
    if shift < 0:
        return jnp.concatenate([zero, field[:, :56]], axis=1)
    if shift > 0:
        return jnp.concatenate([field[:, 8:], zero], axis=1)
    return field


def widen(store, field):
    lane = lane_of((512, 128))
    zero = jnp.zeros((64, 1152), BF16)
    near = [
        jnp.where(lane >= 64, pltpu.roll(field[:, 256:384], 64, 1), 0.0),
        jnp.where(lane < 64, pltpu.roll(field[:, 128:256], 64, 1), 0.0),
    ]
    for half in range(2):
        store[half, 0] = zero
        store[half, 9] = zero
        whole = jnp.concatenate([field[:, half * 256 : half * 256 + 256], near[half]], axis=1)
        whole = whole.reshape(8, 64, 384)
        for j in range(3):
            store[half, 1:9, :, j * 384 : (j + 1) * 384] = shift_y(whole, j - 1).astype(BF16)


def rows_of(store, half, i):
    return store[half, i : i + 8].reshape(512, 1152)


def place_weights(w_hidden, ahead, back):
    lane = lane_of((64, 128))
    low = lane < 64
    zero = jnp.zeros((64, 128), BF16)
    tiles = [w_hidden[:, t * 128 : (t + 1) * 128] for t in range(13)]
    last = w_hidden[:, 1664:1728]
    tiles.append(jnp.concatenate([last, last], axis=1))
    tiles = [t.astype(F32) for t in tiles]
    swapped = [pltpu.roll(t, 64, 1) for t in tiles]
    for j in range(9):
        t = 3 * j // 2
        if j % 2 == 0:
            ab = tiles[t]
            bc = jnp.where(low, swapped[t], swapped[t + 1])
            c_low, c_high = tiles[t + 1], swapped[t + 1]
            a_low, a_high = tiles[t], swapped[t]
        else:
            bc = tiles[t + 1]
            ab = jnp.where(low, swapped[t], swapped[t + 1])
            c_low, c_high = swapped[t + 1], tiles[t + 1]
            a_low, a_high = swapped[t], tiles[t]
        c_0 = jnp.where(low, c_low, 0.0).astype(BF16)
        o_c = jnp.where(low, 0.0, c_high).astype(BF16)
        a_0 = jnp.where(low, a_low, 0.0).astype(BF16)
        o_a = jnp.where(low, 0.0, a_high).astype(BF16)
        ab = ab.astype(BF16)
        bc = bc.astype(BF16)
        rows = [(bc, zero, a_0), (ab, c_0, zero), (o_a, bc, zero), (zero, ab, o_c)]
        for zo in range(4):
            for part in range(3):
                start = (j % 3) * 384 + part * 128
                ahead[j // 3, zo * 64 : (zo + 1) * 64, start : start + 128] = rows[zo][part]
        flip = 8 - j
        rows = [(bc, zero), (ab, c_0), (o_a, bc), (zero, ab), (c_0, zero), (zero, o_a)]
        for zi in range(6):
            start = (flip % 3) * 384 + zi * 64
            for part in range(2):
                back[flip // 3, start : start + 64, part * 128 : (part + 1) * 128] = rows[zi][part]


def whole_kernel(*refs):
    sources, refs = refs[:9], refs[9:]
    (u_next, slot_loss, grad_first, grad_hidden, grad_last), refs = refs[:5], refs[5:]
    held_in, refs = refs[:9], refs[9:]
    vel, target, w_first, w_hidden, w_last, owner, block, fixed, sel = held_in
    (
        filt, first_in, w_one, ahead, back, wide_act, wide_del, slope_one, eddy_z,
        sums, first_sums, ext, y_out, y_in, z_out, z_in,
        half_in, half_sum, chunk_in, chunk_sum, deep_in, total,
        f_in, f_sum, f_plane, f_mid, f_deep, f_total,
        local_sems, sems,
    ) = refs

    loads = [
        pltpu.make_async_copy(src, dst, local_sems.at[n])
        for n, (src, dst) in enumerate(zip(sources, held_in))
    ]
    for n in (3, 0, 2, 8, 7, 1, 4, 5, 6):
        loads[n].start()

    gx, gy, role = lax.axis_index("gx"), lax.axis_index("gy"), lax.axis_index("role")
    depth, y = gx // 4, gx % 4
    x, core = (gy // 2) * 2 + role, gy % 2
    spot = y * 4 + x

    def plane(dy, dx):
        to_y, to_x = (y + dy) % 4, (x + dx) % 4
        return to_y * 4 + to_x, (depth * 4 + to_y, (to_x // 2) * 2 + core, to_x % 2)

    steps = [(dy, dx) for dy in range(4) for dx in range(4) if dy or dx]
    deeper = [(((depth + d) % 8) * 4 + y, gy, role) for d in range(1, 8)]
    other = (gx, gy - core + 1 - core, role)
    x_up, x_down = ((gx + 1) % 32, gy, role), ((gx + 31) % 32, gy, role)
    y_up, y_down = (gx, (gy + 1) % 4, role), (gx, (gy + 3) % 4, role)
    z_side = (gx, gy, 1 - role)

    barrier = pltpu.get_barrier_semaphore()
    greeted = [plane(dy, dx)[1] for dy, dx in steps] + deeper + [x_up, x_down, y_up, y_down]
    for device in greeted:
        pl.semaphore_signal(barrier, inc=1, device_id=device, device_id_type=MESH)

    started = []

    def send(src, dst, device):
        at = len(started)
        part = pltpu.make_async_remote_copy(
            src_ref=src, dst_ref=dst, send_sem=sems.at[0, at], recv_sem=sems.at[1, at],
            device_id=device, device_id_type=MESH,
        )
        started.append(part)
        part.start()
        return part

    loads[3].wait()
    place_weights(w_hidden, ahead, back)
    loads[2].wait()
    loads[8].wait()
    placed = dot(w_first[...], sel[...]).astype(BF16)
    for i in range(3):
        for zo in range(8):
            at = (i * 8 + zo) * 128
            w_one[i, zo * 64 : (zo + 1) * 64, :] = placed[:, at : at + 128]

    for n in (0, 7, 1, 4, 5, 6):
        loads[n].wait()
    pooled = []
    for comp in range(3):
        summed = None
        for dx in range(2):
            for dy in range(2):
                part = jnp.concatenate(
                    [vel[comp, 2 * i + dx, pl.ds(dy, 8, stride=2), :] for i in range(8)], axis=0
                )
                summed = part if summed is None else summed + part
        pooled.append(summed)
    rest = jnp.concatenate(pooled, axis=1)
    blocks = None
    for _ in range(3):
        piece = rest.astype(BF16)
        rest = rest - piece.astype(F32)
        term = dot(piece, fixed[0:384])
        blocks = term if blocks is None else blocks + term
    blocks = blocks.astype(BF16).astype(F32)
    want = target[...].astype(F32).reshape(64, 64).astype(BF16)
    blocks = blocks + dot(want, fixed[384:448])
    for b in range(8):
        tile = blocks[:, (b // 4) * 128 : (b // 4) * 128 + 128]
        if b % 4:
            tile = pltpu.roll(tile, 128 - 32 * (b % 4), 1)
        filt[pl.ds(b, 64, stride=8), :] = tile
    held = filt[...]
    held16 = held.astype(BF16)
    targets = jnp.concatenate([dot(held16, fixed[448:576]), dot(held16, fixed[576:704])], axis=1)
    lane = lane_of((512, 128))
    inputs = jnp.where(lane < 24, held, 0.0).reshape(8, 64, 128)
    near = shift_y(inputs, -1)
    near = near + pltpu.roll(inputs.reshape(512, 128), 32, 1).reshape(8, 64, 128)
    near = near + pltpu.roll(shift_y(inputs, 1).reshape(512, 128), 64, 1).reshape(8, 64, 128)
    first_in[0] = jnp.zeros((64, 128), BF16)
    first_in[9] = jnp.zeros((64, 128), BF16)
    first_in[1:9] = near.astype(BF16)

    pre = None
    for i in range(3):
        term = dot(first_in[i : i + 8].reshape(512, 128), w_one[i], NT)
        pre = term if pre is None else pre + term
    sig = 1.0 / (1.0 + jnp.exp(-pre))
    slope_one[...] = sig * (1.0 + pre * (1.0 - sig))
    widen(wide_act, (pre * sig).astype(BF16).astype(F32))

    slot_of, base_of = (0, 0, 1, 2), (0, 16, 0, 0)
    lane16 = lane_of((16, 128))

    def pack_sides(c, field, wide):
        for h in range(wide):
            for i in range(16):
                low, high = field[i, h : h + 1, :], field[i, 16 - wide + h : 17 - wide + h, :]
                y_out[0, 2 * c + h, i : i + 1, :] = low
                y_out[1, 2 * c + h, i : i + 1, :] = high
        packed = None
        for i in range(16):
            g = base_of[c] + i
            moved = pltpu.roll(field[i], 2 + 4 * g, 1)
            packed = moved if packed is None else jnp.where(lane16 // 4 == g, moved, packed)
        return packed

    sides_of = [pack_sides(c, vel.at[c], 2) for c in range(3)]
    z_out[0] = jnp.where(lane16 < 64, sides_of[0], sides_of[1])
    z_out[1] = sides_of[2]

    wl = w_last[...].astype(F32)
    wl = jnp.concatenate([wl, wl, wl, wl], axis=1)
    rows_iota = lax.broadcasted_iota(jnp.int32, (384, 256), 0)
    lanes_iota = lax.broadcasted_iota(jnp.int32, (384, 256), 1)
    cell = jnp.where(rows_iota < 256, rows_iota // 64, (rows_iota // 2) % 4)
    out_map = jnp.where(cell == lanes_iota // 64, wl, 0.0).astype(BF16)

    number = lax.broadcasted_iota(jnp.int32, (8, 256), 0)
    drawn = jnp.where((owner[...] == gx) & (block[...] == number), 1.0, 0.0)
    times = jnp.sum(drawn, axis=1, keepdims=True)

    loss = jnp.zeros((8, 256), F32)
    last = jnp.zeros((8, 256), F32)
    deltas, parts = [], []
    for half in range(2):
        pre = None
        for i in range(3):
            term = dot(rows_of(wide_act, half, i), ahead[i], NT)
            pre = term if pre is None else pre + term
        sig = 1.0 / (1.0 + jnp.exp(-pre))
        act = (pre * sig).astype(BF16)
        slope = sig * (1.0 + pre * (1.0 - sig))
        both = dot(act, out_map, NT)
        logits = both[:, :256]
        eddy_z[half] = 0.5 * (
            jnp.maximum(both[:, 256:], 0.0) + jnp.log1p(jnp.exp(-jnp.abs(both[:, 256:])))
        )
        small = jnp.exp(-jnp.abs(logits))
        eddy = 0.5 * (jnp.maximum(logits, 0.0) + jnp.log1p(small))
        gate = jnp.where(logits >= 0, 1.0, small) / (1.0 + small)
        error = eddy - targets[:, half * 256 : half * 256 + 256]
        loss = loss + jnp.sum((error * error).reshape(64, 8, 256), axis=0)
        d_logit = (error * gate * (1.0 / (256 * 512))).astype(BF16).astype(F32)
        last = last + jnp.sum((d_logit * act.astype(F32)).reshape(64, 8, 256), axis=0)
        delta = (wl * d_logit * slope).astype(BF16).astype(F32)
        deltas.append(delta)
        scaled = (delta.reshape(64, 8, 256) * times.reshape(1, 8, 1)).reshape(512, 256)
        low = scaled - scaled.astype(BF16).astype(F32)
        parts.append(jnp.concatenate([scaled.T.astype(BF16), low.T.astype(BF16)], axis=0))
    widen(wide_del, jnp.concatenate(deltas, axis=1))

    lane = lane_of((64, 128))
    field = jnp.zeros((64, 128), F32)
    for half in range(2):
        for b in range(8):
            part = eddy_z[half, pl.ds(b, 64, stride=8), :]
            field = jnp.where(lane // 8 == 2 * b + half, part, field)
    field = 0.02 + field
    for i in range(8):
        for dx in range(2):
            for dy in range(2):
                ext[3, 2 + 2 * i + dx, pl.ds(8 + dy, 8, stride=2), :] = field[i * 8 : i * 8 + 8]
    z_out[2] = pack_sides(3, ext.at[3, 2:18, 8:24], 1)
    pl.semaphore_wait(barrier, len(greeted))
    rims = [
        send(vel.at[:, 0:2], ext.at[0:3, 18:20, 8:24], x_down),
        send(vel.at[:, 14:16], ext.at[0:3, 0:2, 8:24], x_up),
        send(ext.at[3, 2:3, 8:24], ext.at[3, 18:19, 8:24], x_down),
        send(ext.at[3, 17:18, 8:24], ext.at[3, 1:2, 8:24], x_up),
        send(y_out.at[0], y_in.at[1], y_down),
        send(y_out.at[1], y_in.at[0], y_up),
        send(z_out, z_in, z_side),
    ]

    per_block = jnp.sum(loss, axis=1, keepdims=True) * (1.0 / (64 * 512))
    by_slot = jnp.sum(drawn * per_block, axis=0, keepdims=True)
    group = gy * 2 + role
    at = lax.broadcasted_iota(jnp.int32, (64, 128), 0)
    by_slot = jnp.where(at % 2 == 0, by_slot[:, :128], by_slot[:, 128:])
    sums[0, 448:512, :] = jnp.where(at // 2 == group, by_slot, 0.0)
    last = jnp.sum(last * times, axis=0, keepdims=True)
    last = last[:, :128] + last[:, 128:]
    last = last + pltpu.roll(last, 64, 1)
    sums[1, 448:512, :] = jnp.broadcast_to(last, (64, 128))

    def column(t, value):
        sums[t // 7, (t % 7) * 64 : (t % 7) * 64 + 64, :] = value

    is_low = lane < 64
    held_a = None
    for i in range(3):
        grad = None
        for half in range(2):
            term = dot(parts[half], rows_of(wide_act, half, i))
            grad = term if grad is None else grad + term
        grad = grad[:256] + grad[256:]
        for j in range(3):
            k = 3 * i + j
            g = [
                [grad[zo * 64 : zo * 64 + 64, j * 384 + p * 128 : j * 384 + p * 128 + 128] for p in range(3)]
                for zo in range(4)
            ]
            bc = g[0][0] + g[2][1]
            ab = g[1][0] + g[3][1]
            cb = pltpu.roll(bc, 64, 1)
            a_low = g[0][2] + pltpu.roll(g[2][0], 64, 1)
            ab = ab + jnp.where(is_low, a_low, cb)
            c_low = cb + g[1][1] + pltpu.roll(g[3][2], 64, 1)
            t = 3 * k // 2
            if k % 2 == 0:
                column(t, ab)
                held_a = c_low
            else:
                ba = pltpu.roll(ab, 64, 1)
                column(t, jnp.where(is_low, held_a, ba))
                column(t + 1, jnp.where(is_low, ba, pltpu.roll(c_low, 64, 1)))
    column(13, jnp.where(is_low, held_a, 0.0))
    first = send(sums.at[1 - core], half_in, other)

    firsts = []
    scatter = []
    for half in range(2):
        d_act = None
        for i in range(3):
            term = dot(rows_of(wide_del, half, i), back[i])
            d_act = term if d_act is None else d_act + term
        d_first = (d_act * slope_one[:, half * 256 : half * 256 + 256]).astype(BF16).astype(F32)
        scaled = (d_first.reshape(64, 8, 256) * times.reshape(1, 8, 1)).reshape(512, 256)
        low = scaled - scaled.astype(BF16).astype(F32)
        firsts.append((scaled.T.astype(BF16), low.T.astype(BF16)))
        if half == 0:
            first.wait_recv()
            half_sum[...] = sums[core] + half_in[...]
            for s, (dy, dx) in enumerate(steps):
                to, device = plane(dy, dx)
                scatter.append(
                    send(half_sum.at[pl.ds(pl.multiple_of(to * 32, 32), 32)], chunk_in.at[s], device)
                )
    lhs = jnp.concatenate([firsts[0][0], firsts[1][0], firsts[0][1], firsts[1][1]], axis=0)
    packed = jnp.zeros((64, 128), F32)
    for i in range(3):
        grad = dot(lhs, first_in[i : i + 8].reshape(512, 128))
        grad = grad[:512] + grad[512:]
        summed = None
        for zo in range(8):
            part = grad[zo * 64 : zo * 64 + 64]
            shift = (-3 * (zo - 1)) % 128
            part = pltpu.roll(part, shift, 1) if shift else part
            summed = part if summed is None else summed + part
        for j in range(3):
            start = 9 * (3 * i + j)
            shift = (start - 32 * j) % 128
            moved = pltpu.roll(summed, shift, 1) if shift else summed
            packed = jnp.where((lane >= start) & (lane < start + 9), moved, packed)
    first_sums[...] = packed

    own32 = pl.ds(pl.multiple_of(core * 32, 32), 32)
    f_first = send(
        first_sums.at[pl.ds(pl.multiple_of((1 - core) * 32, 32), 32)], f_in, other
    )
    ext[0:3, 2:18, 8:24, :] = vel[...]
    f_first.wait_recv()
    mine = first_sums[own32, :] + f_in[...]
    f_sum[...] = mine
    f_plane[spot] = mine
    f_across = [send(f_sum, f_plane.at[spot], plane(dy, dx)[1]) for dy, dx in steps]

    for part in scatter:
        part.wait_recv()
    mine = half_sum[pl.ds(pl.multiple_of(spot * 32, 32), 32), :]
    for s in range(15):
        mine = mine + chunk_in[s]
    chunk_sum[...] = mine
    deep_in[depth] = mine
    deep = [send(chunk_sum, deep_in.at[depth], device) for device in deeper]

    for rim in rims:
        rim.wait_recv()
    for c in range(4):
        for h in range(1 if c == 3 else 2):
            for i in range(16):
                to = 7 if c == 3 else 6 + h
                ext[c, 2 + i, to : to + 1, :] = y_in[0, 2 * c + h, i : i + 1, :]
                ext[c, 2 + i, 24 + h : 25 + h, :] = y_in[1, 2 * c + h, i : i + 1, :]

    def row(i, carry):
        def beside(c, here, far):
            turn = (254 - 4 * (base_of[c] + i)) % 128
            edge = pltpu.roll(z_in[slot_of[c]], turn, 1)
            out = []
            for m in (1, 2) if far else (1,):
                after = jnp.where(lane16 < m, edge, here)
                before = jnp.where(lane16 >= 128 - m, edge, here)
                out += [pltpu.roll(after, 128 - m, 1), pltpu.roll(before, m, 1)]
            return out

        centre = ext[3, 2 + i, 8:24, :]
        sides = [
            (ext[3, 3 + i, 8:24, :], ext[3, 1 + i, 8:24, :]),
            (ext[3, 2 + i, 9:25, :], ext[3, 2 + i, 7:23, :]),
            beside(3, centre, False),
        ]
        sides = [(0.5 * (centre + a), 0.5 * (centre + b)) for a, b in sides]
        speed = [ext[c, 2 + i, 8:24, :] for c in range(3)]
        for c in range(3):
            here = speed[c]
            near = [
                [ext[c, 2 + i + m, 8:24, :] for m in (1, -1, 2, -2)],
                [ext[c, 2 + i, 8 + m : 24 + m, :] for m in (1, -1, 2, -2)],
                beside(c, here, True),
            ]
            change = None
            for axis in range(3):
                a1, b1, a2, b2 = near[axis]
                slope = (8.0 * (a1 - b1) - (a2 - b2)) * (1.0 / 12.0)
                term = sides[axis][0] * (a1 - here) - sides[axis][1] * (here - b1)
                term = term - speed[axis] * slope
                change = term if change is None else change + term
            u_next[c, i] = here + 0.2 * change
        return carry

    lax.fori_loop(0, 16, row, 0)

    for part in f_across:
        part.wait_recv()
    mine = f_plane[0]
    for s in range(1, 16):
        mine = mine + f_plane[s]
    f_mid[...] = mine
    f_deep[depth] = mine
    f_planes = [send(f_mid, f_deep.at[depth], device) for device in deeper]

    for part in deep:
        part.wait_recv()
    mine = deep_in[0]
    for d in range(1, 8):
        mine = mine + deep_in[d]
    own = pl.ds(pl.multiple_of(spot * 32, 32), 32)
    total[core, own, :] = mine
    gather = [
        send(total.at[core, own], total.at[core, own], plane(dy, dx)[1]) for dy, dx in steps
    ]

    for part in f_planes:
        part.wait_recv()
    mine = f_deep[0]
    for d in range(1, 8):
        mine = mine + f_deep[d]
    f_total[own32, :] = mine
    f_last = send(f_total.at[own32], f_total.at[own32], other)

    across = []
    for dy in range(4):
        for part, (sy, _) in zip(gather, steps):
            if sy == dy:
                part.wait_recv()
        rows = pl.ds(pl.multiple_of(((y + 4 - dy) % 4) * 128, 128), 128)
        across.append(send(total.at[core, rows], total.at[core, rows], other))
    f_last.wait_recv()
    grad_first[...] = f_total[:, :81]
    for part in across:
        part.wait_recv()

    for t in range(14):
        wide = 64 if t == 13 else 128
        grad_hidden[:, t * 128 : t * 128 + wide] = total[t // 7, (t % 7) * 64 : (t % 7) * 64 + 64, :wide]
    grad_last[...] = total[1, 448:449, :64]
    losses = total[0, 448:464, :]
    at = lax.broadcasted_iota(jnp.int32, (16, 128), 0)
    losses = jnp.where(at == (gy * 2 + role) * 2 + gx // 16, losses, 0.0)
    losses = jnp.sum(losses, axis=0, keepdims=True)
    losses = pltpu.roll(losses, (128 - (gx % 16) * 8) % 128, 1)
    slot_loss[0] = losses[:, :8]
    for part in started:
        part.wait_send()


SENDS = 7 + 1 + 15 + 1 + 15 + 7 + 7 + 15 + 1 + 4


def out_shapes():
    return (
        jax.ShapeDtypeStruct((3, 16, 16, 128), F32),
        jax.ShapeDtypeStruct((1, 1, 8), F32),
        jax.ShapeDtypeStruct((64, 81), F32),
        jax.ShapeDtypeStruct((64, 1728), F32),
        jax.ShapeDtypeStruct((1, 64), F32),
    )


def hand_out(*refs):
    moves = [pltpu.make_async_copy(refs[n], refs[5 + n], refs[10].at[n]) for n in range(5)]
    for move in moves:
        move.start()
    for move in moves:
        move.wait()


def on_device(velocity, target_visc, w_first, w_hidden, w_last, sample_owner, sample_block):
    vmem = pl.BlockSpec(memory_space=pltpu.VMEM)
    far = pl.BlockSpec(memory_space=pltpu.HBM)
    spread = spread_matrix()
    rows = (pool_matrix(), target_matrix(), spread[:, :256], spread[:, 256:], spread[:8, :256])
    consts = [jnp.asarray(np.concatenate(rows, 0)), jnp.asarray(first_selector())]
    args = [
        velocity, target_visc, w_first, w_hidden, w_last.reshape(1, 64),
        sample_owner.reshape(1, 256), sample_block.reshape(1, 256), *consts,
    ]
    outs = pl.pallas_call(
        whole_kernel,
        out_shape=out_shapes(),
        in_specs=[far] * 9,
        out_specs=(vmem,) * 5,
        scratch_shapes=[pltpu.VMEM(a.shape, a.dtype) for a in args] + [
            pltpu.VMEM((512, 128), F32),
            pltpu.VMEM((10, 64, 128), BF16),
            pltpu.VMEM((3, 512, 128), BF16),
            pltpu.VMEM((3, 256, 1152), BF16),
            pltpu.VMEM((3, 1152, 256), BF16),
            pltpu.VMEM((2, 10, 64, 1152), BF16),
            pltpu.VMEM((2, 10, 64, 1152), BF16),
            pltpu.VMEM((512, 512), F32),
            pltpu.VMEM((2, 512, 128), F32),
            pltpu.VMEM((2, 512, 128), F32),
            pltpu.VMEM((64, 128), F32),
            pltpu.VMEM((4, 20, 32, 128), F32),
            pltpu.VMEM((2, 7, 16, 128), F32),
            pltpu.VMEM((2, 7, 16, 128), F32),
            pltpu.VMEM((3, 16, 128), F32),
            pltpu.VMEM((3, 16, 128), F32),
            pltpu.VMEM((512, 128), F32),
            pltpu.VMEM((512, 128), F32),
            pltpu.VMEM((15, 32, 128), F32),
            pltpu.VMEM((32, 128), F32),
            pltpu.VMEM((8, 32, 128), F32),
            pltpu.VMEM((2, 512, 128), F32),
            pltpu.VMEM((32, 128), F32),
            pltpu.VMEM((32, 128), F32),
            pltpu.VMEM((16, 32, 128), F32),
            pltpu.VMEM((32, 128), F32),
            pltpu.VMEM((8, 32, 128), F32),
            pltpu.VMEM((64, 128), F32),
            pltpu.SemaphoreType.DMA((9,)),
            pltpu.SemaphoreType.DMA((2, SENDS)),
        ],
        compiler_params=pltpu.CompilerParams(
            vmem_limit_bytes=48 * 1024 * 1024, collective_id=0, has_side_effects=True
        ),
        name="whole",
    )(*args)
    outs = pl.pallas_call(
        hand_out,
        out_shape=out_shapes(),
        in_specs=[vmem] * 5,
        out_specs=(far,) * 5,
        scratch_shapes=[pltpu.SemaphoreType.DMA((5,))],
        compiler_params=pltpu.CompilerParams(vmem_limit_bytes=8 * 1024 * 1024),
        name="hand_out",
    )(*outs)
    u_next, slot_loss, grad_first, grad_hidden, grad_last = outs
    return (u_next, slot_loss, grad_first, grad_hidden, grad_last.reshape(64))


def solution(mesh):
    return jax.shard_map(
        on_device,
        mesh=mesh,
        in_specs=(
            P(None, "gx", "gy", "role"),
            P("gx", "gy", "role"),
            P(),
            P(),
            P(),
            P("gy", "role", None, None),
            P("gy", "role", None, None),
        ),
        out_specs=(P(None, "gx", "gy", "role"), P("gy", "role", "gx"), P(), P(), P()),
        check_vma=False,
    )
```

```python
import numpy as np
import jax
import jax.numpy as jnp
from jax import lax
from jax.sharding import PartitionSpec as P
from jax.experimental import pallas as pl
from jax.experimental.pallas import tpu as pltpu

SIDE = 8
CH = 64
F32 = jnp.float32
BF16 = jnp.bfloat16
NT = (((1,), (1,)), ((), ()))
NN = (((1,), (0,)), ((), ()))
MESH = pl.DeviceIdType.MESH


def dot(a, b, dims=NN):
    return lax.dot_general(a, b, dims, preferred_element_type=F32)


def pool_matrix():
    z = np.arange(128)[:, None]
    lane = np.arange(256)[None, :]
    block, inner = lane // 32, lane % 32
    parts = []
    for comp in range(3):
        hit = (inner < 24) & (inner % 3 == comp) & (z // 2 == block * 8 + inner // 3)
        parts.append(np.where(hit, 0.125, 0.0))
    return np.concatenate(parts, 0).astype(jnp.bfloat16)


def target_matrix():
    z = np.arange(64)[:, None]
    lane = np.arange(256)[None, :]
    block, inner = lane // 32, lane % 32
    return ((inner >= 24) & (z == block * 8 + inner - 24)).astype(jnp.bfloat16)


def spread_matrix():
    row = np.arange(128)[:, None]
    lane = np.arange(512)[None, :]
    return (row == 24 + lane // 64).astype(jnp.bfloat16)


def first_selector():
    out = np.zeros((81, 3, 8, 128), np.float32)
    for i in range(3):
        for zo in range(8):
            for j in range(3):
                for t in range(9):
                    zi = zo - 1 + t // 3
                    if 0 <= zi < 8:
                        out[9 * (3 * i + j) + t, i, zo, j * 32 + zi * 3 + t % 3] = 1.0
    return out.reshape(81, 3072).astype(jnp.bfloat16)


def lane_of(shape):
    return lax.broadcasted_iota(jnp.int32, shape, len(shape) - 1)


def shift_y(field, shift):
    zero = jnp.zeros((8, 8, field.shape[2]), field.dtype)
    if shift < 0:
        return jnp.concatenate([zero, field[:, :56]], axis=1)
    if shift > 0:
        return jnp.concatenate([field[:, 8:], zero], axis=1)
    return field


def widen(store, field):
    lane = lane_of((512, 128))
    zero = jnp.zeros((64, 1152), BF16)
    near = [
        jnp.where(lane >= 64, pltpu.roll(field[:, 256:384], 64, 1), 0.0),
        jnp.where(lane < 64, pltpu.roll(field[:, 128:256], 64, 1), 0.0),
    ]
    for half in range(2):
        store[half, 0] = zero
        store[half, 9] = zero
        whole = jnp.concatenate([field[:, half * 256 : half * 256 + 256], near[half]], axis=1)
        whole = whole.reshape(8, 64, 384)
        for j in range(3):
            store[half, 1:9, :, j * 384 : (j + 1) * 384] = shift_y(whole, j - 1).astype(BF16)


def widen_pairs(store, field):
    low = lane_of((512, 128)) < 64
    zero = jnp.zeros((64, 768), BF16)
    none = jnp.zeros((512, 128), F32)
    pairs = [field[:, p * 128 : (p + 1) * 128] for p in range(4)]
    turned = [none] + [pltpu.roll(p, 64, 1) for p in pairs] + [none]
    for p in range(4):
        store[p, 0] = zero
        store[p, 9] = zero
        near = jnp.where(low, turned[p], turned[p + 2])
        whole = jnp.concatenate([pairs[p], near], axis=1).reshape(8, 64, 256)
        for j in range(3):
            store[p, 1:9, :, j * 256 : (j + 1) * 256] = shift_y(whole, j - 1).astype(BF16)


def rows_of(store, half, i):
    return store[half, i : i + 8].reshape(512, 1152)


def place_weights(w_hidden, ahead, back):
    lane = lane_of((64, 128))
    low = lane < 64
    zero = jnp.zeros((64, 128), BF16)
    tiles = [w_hidden[:, t * 128 : (t + 1) * 128] for t in range(13)]
    last = w_hidden[:, 1664:1728]
    tiles.append(jnp.concatenate([last, last], axis=1))
    tiles = [t.astype(F32) for t in tiles]
    swapped = [pltpu.roll(t, 64, 1) for t in tiles]
    for j in range(9):
        t = 3 * j // 2
        if j % 2 == 0:
            ab = tiles[t]
            bc = jnp.where(low, swapped[t], swapped[t + 1])
            c_low, c_high = tiles[t + 1], swapped[t + 1]
            a_low, a_high = tiles[t], swapped[t]
        else:
            bc = tiles[t + 1]
            ab = jnp.where(low, swapped[t], swapped[t + 1])
            c_low, c_high = swapped[t + 1], tiles[t + 1]
            a_low, a_high = swapped[t], tiles[t]
        c_0 = jnp.where(low, c_low, 0.0).astype(BF16)
        o_c = jnp.where(low, 0.0, c_high).astype(BF16)
        a_0 = jnp.where(low, a_low, 0.0).astype(BF16)
        o_a = jnp.where(low, 0.0, a_high).astype(BF16)
        ab = ab.astype(BF16)
        bc = bc.astype(BF16)
        rows = [(bc, zero, a_0), (ab, c_0, zero), (o_a, bc, zero), (zero, ab, o_c)]
        for zo in range(4):
            for part in range(3):
                start = (j % 3) * 384 + part * 128
                ahead[j // 3, zo * 64 : (zo + 1) * 64, start : start + 128] = rows[zo][part]
        flip = 8 - j
        rows = [(bc, zero), (ab, c_0), (o_a, bc), (zero, ab), (c_0, zero), (zero, o_a)]
        for zi in range(6):
            start = (flip % 3) * 384 + zi * 64
            for part in range(2):
                back[flip // 3, start : start + 64, part * 128 : (part + 1) * 128] = rows[zi][part]


def whole_kernel(*refs):
    sources, refs = refs[:9], refs[9:]
    results, refs = refs[:5], refs[5:]
    held_in, refs = refs[:9], refs[9:]
    vel, target, w_first, w_hidden, w_last, owner, block, fixed, sel = held_in
    held_out, refs = refs[:5], refs[5:]
    u_next, slot_loss, grad_first, grad_hidden, grad_last = held_out
    (
        filt, first_in, w_one, ahead, back, wide_act, wide_del, slope_one, pair_act, eddy_z,
        sums, first_sums, ext, y_out, y_in, z_out, z_in,
        half_in, half_sum, chunk_in, chunk_sum, deep_in, total,
        f_in, f_sum, f_plane, f_mid, f_deep, f_total,
        local_sems, sems,
    ) = refs

    loads = [
        pltpu.make_async_copy(src, dst, local_sems.at[n])
        for n, (src, dst) in enumerate(zip(sources, held_in))
    ]
    for n in (3, 0, 2, 8, 7, 1, 4, 5, 6):
        loads[n].start()

    def hand_over(n):
        move = pltpu.make_async_copy(held_out[n], results[n], local_sems.at[9 + n])
        move.start()
        return move

    gx, gy, role = lax.axis_index("gx"), lax.axis_index("gy"), lax.axis_index("role")
    depth, y = gx // 4, gx % 4
    x, core = (gy // 2) * 2 + role, gy % 2
    spot = y * 4 + x

    def plane(dy, dx):
        to_y, to_x = (y + dy) % 4, (x + dx) % 4
        return to_y * 4 + to_x, (depth * 4 + to_y, (to_x // 2) * 2 + core, to_x % 2)

    reach = (0, 1, 2, 1)
    steps = [(dy, dx) for dy in range(4) for dx in range(4) if dy or dx]
    steps.sort(key=lambda s: -reach[s[0]] - reach[s[1]])
    deeper = [(((depth + d) % 8) * 4 + y, gy, role) for d in (4, 3, 5, 2, 6, 1, 7)]
    other = (gx, gy - core + 1 - core, role)
    x_up, x_down = ((gx + 1) % 32, gy, role), ((gx + 31) % 32, gy, role)
    y_up, y_down = (gx, (gy + 1) % 4, role), (gx, (gy + 3) % 4, role)
    z_side = (gx, gy, 1 - role)

    barrier = pltpu.get_barrier_semaphore()
    greeted = [plane(dy, dx)[1] for dy, dx in steps] + deeper + [x_up, x_down, y_up, y_down]
    for device in greeted:
        pl.semaphore_signal(barrier, inc=1, device_id=device, device_id_type=MESH)

    started = []

    def send(src, dst, device):
        at = len(started)
        part = pltpu.make_async_remote_copy(
            src_ref=src, dst_ref=dst, send_sem=sems.at[0, at], recv_sem=sems.at[1, at],
            device_id=device, device_id_type=MESH,
        )
        started.append(part)
        part.start()
        return part

    loads[3].wait()
    place_weights(w_hidden, ahead, back)
    loads[2].wait()
    loads[8].wait()
    placed = dot(w_first[...], sel[...]).astype(BF16)
    for i in range(3):
        for zo in range(8):
            at = (i * 8 + zo) * 128
            w_one[i, zo * 64 : (zo + 1) * 64, :] = placed[:, at : at + 128]

    for n in (0, 7, 1, 4, 5, 6):
        loads[n].wait()
    pooled = []
    for comp in range(3):
        summed = None
        for dx in range(2):
            for dy in range(2):
                part = jnp.concatenate(
                    [vel[comp, 2 * i + dx, pl.ds(dy, 8, stride=2), :] for i in range(8)], axis=0
                )
                summed = part if summed is None else summed + part
        pooled.append(summed)
    rest = jnp.concatenate(pooled, axis=1)
    blocks = None
    for _ in range(3):
        piece = rest.astype(BF16)
        rest = rest - piece.astype(F32)
        term = dot(piece, fixed[0:384])
        blocks = term if blocks is None else blocks + term
    blocks = blocks.astype(BF16).astype(F32)
    want = target[...].astype(F32).reshape(64, 64).astype(BF16)
    blocks = blocks + dot(want, fixed[384:448])
    for b in range(8):
        tile = blocks[:, (b // 4) * 128 : (b // 4) * 128 + 128]
        if b % 4:
            tile = pltpu.roll(tile, 128 - 32 * (b % 4), 1)
        filt[pl.ds(b, 64, stride=8), :] = tile
    held = filt[...]
    held16 = held.astype(BF16)
    targets = jnp.concatenate([dot(held16, fixed[448:576]), dot(held16, fixed[576:704])], axis=1)
    lane = lane_of((512, 128))
    inputs = jnp.where(lane < 24, held, 0.0).reshape(8, 64, 128)
    near = shift_y(inputs, -1)
    near = near + pltpu.roll(inputs.reshape(512, 128), 32, 1).reshape(8, 64, 128)
    near = near + pltpu.roll(shift_y(inputs, 1).reshape(512, 128), 64, 1).reshape(8, 64, 128)
    first_in[0] = jnp.zeros((64, 128), BF16)
    first_in[9] = jnp.zeros((64, 128), BF16)
    first_in[1:9] = near.astype(BF16)

    pre = None
    for i in range(3):
        term = dot(first_in[i : i + 8].reshape(512, 128), w_one[i], NT)
        pre = term if pre is None else pre + term
    sig = 1.0 / (1.0 + jnp.exp(-pre))
    slope_one[...] = sig * (1.0 + pre * (1.0 - sig))
    acts = (pre * sig).astype(BF16).astype(F32)
    widen(wide_act, acts)
    widen_pairs(pair_act, acts)

    slot_of, base_of = (0, 0, 1, 2), (0, 16, 0, 0)
    lane16 = lane_of((16, 128))

    def pack_sides(c, field, wide):
        for h in range(wide):
            for i in range(16):
                low, high = field[i, h : h + 1, :], field[i, 16 - wide + h : 17 - wide + h, :]
                y_out[0, 2 * c + h, i : i + 1, :] = low
                y_out[1, 2 * c + h, i : i + 1, :] = high
        packed = None
        for i in range(16):
            g = base_of[c] + i
            moved = pltpu.roll(field[i], 2 + 4 * g, 1)
            packed = moved if packed is None else jnp.where(lane16 // 4 == g, moved, packed)
        return packed

    sides_of = [pack_sides(c, vel.at[c], 2) for c in range(3)]
    z_out[0] = jnp.where(lane16 < 64, sides_of[0], sides_of[1])
    z_out[1] = sides_of[2]

    wl = w_last[...].astype(F32)
    wl = jnp.concatenate([wl, wl, wl, wl], axis=1)
    rows_iota = lax.broadcasted_iota(jnp.int32, (384, 256), 0)
    lanes_iota = lax.broadcasted_iota(jnp.int32, (384, 256), 1)
    cell = jnp.where(rows_iota < 256, rows_iota // 64, (rows_iota // 2) % 4)
    out_map = jnp.where(cell == lanes_iota // 64, wl, 0.0).astype(BF16)

    number = lax.broadcasted_iota(jnp.int32, (8, 256), 0)
    drawn = jnp.where((owner[...] == gx) & (block[...] == number), 1.0, 0.0)
    times = jnp.sum(drawn, axis=1, keepdims=True)

    loss = jnp.zeros((8, 256), F32)
    last = jnp.zeros((8, 256), F32)
    deltas, parts = [], []
    for half in range(2):
        pre = None
        for i in range(3):
            term = dot(rows_of(wide_act, half, i), ahead[i], NT)
            pre = term if pre is None else pre + term
        sig = 1.0 / (1.0 + jnp.exp(-pre))
        act = (pre * sig).astype(BF16)
        slope = sig * (1.0 + pre * (1.0 - sig))
        both = dot(act, out_map, NT)
        logits = both[:, :256]
        eddy_z[half] = 0.5 * (
            jnp.maximum(both[:, 256:], 0.0) + jnp.log1p(jnp.exp(-jnp.abs(both[:, 256:])))
        )
        small = jnp.exp(-jnp.abs(logits))
        eddy = 0.5 * (jnp.maximum(logits, 0.0) + jnp.log1p(small))
        gate = jnp.where(logits >= 0, 1.0, small) / (1.0 + small)
        error = eddy - targets[:, half * 256 : half * 256 + 256]
        loss = loss + jnp.sum((error * error).reshape(64, 8, 256), axis=0)
        d_logit = (error * gate * (1.0 / (256 * 512))).astype(BF16).astype(F32)
        last = last + jnp.sum((d_logit * act.astype(F32)).reshape(64, 8, 256), axis=0)
        delta = (wl * d_logit * slope).astype(BF16).astype(F32)
        deltas.append(delta)
        scaled = (delta.reshape(64, 8, 256) * times.reshape(1, 8, 1)).reshape(512, 256)
        high = scaled.astype(BF16)
        low = (scaled - high.astype(F32)).astype(BF16)
        for p in range(2):
            cut = slice(p * 128, p * 128 + 128)
            parts.append(jnp.concatenate([high[:, cut].T, low[:, cut].T], axis=0))
    widen(wide_del, jnp.concatenate(deltas, axis=1))

    lane = lane_of((64, 128))
    field = jnp.zeros((64, 128), F32)
    for half in range(2):
        for b in range(8):
            part = eddy_z[half, pl.ds(b, 64, stride=8), :]
            field = jnp.where(lane // 8 == 2 * b + half, part, field)
    field = 0.02 + field
    for i in range(8):
        for dx in range(2):
            for dy in range(2):
                ext[3, 2 + 2 * i + dx, pl.ds(8 + dy, 8, stride=2), :] = field[i * 8 : i * 8 + 8]
    z_out[2] = pack_sides(3, ext.at[3, 2:18, 8:24], 1)
    pl.semaphore_wait(barrier, len(greeted))
    rims = [
        send(vel.at[:, 0:2], ext.at[0:3, 18:20, 8:24], x_down),
        send(vel.at[:, 14:16], ext.at[0:3, 0:2, 8:24], x_up),
        send(ext.at[3, 2:3, 8:24], ext.at[3, 18:19, 8:24], x_down),
        send(ext.at[3, 17:18, 8:24], ext.at[3, 1:2, 8:24], x_up),
        send(y_out.at[0], y_in.at[1], y_down),
        send(y_out.at[1], y_in.at[0], y_up),
        send(z_out, z_in, z_side),
    ]

    per_block = jnp.sum(loss, axis=1, keepdims=True) * (1.0 / (64 * 512))
    by_slot = jnp.sum(drawn * per_block, axis=0, keepdims=True)
    group = gy * 2 + role
    at = lax.broadcasted_iota(jnp.int32, (64, 128), 0)
    by_slot = jnp.where(at % 2 == 0, by_slot[:, :128], by_slot[:, 128:])
    sums[0, 448:512, :] = jnp.where(at // 2 == group, by_slot, 0.0)
    last = jnp.sum(last * times, axis=0, keepdims=True)
    last = last[:, :128] + last[:, 128:]
    last = last + pltpu.roll(last, 64, 1)
    sums[1, 448:512, :] = jnp.broadcast_to(last, (64, 128))

    def column(t, value):
        sums[t // 7, (t % 7) * 64 : (t % 7) * 64 + 64, :] = value

    is_low = lane < 64
    held_a = None
    for i in range(3):
        grad = None
        for p in range(4):
            term = dot(parts[p], pair_act[p, i : i + 8].reshape(512, 768))
            grad = term if grad is None else grad + term
        grad = grad[:128] + grad[128:]
        for j in range(3):
            k = 3 * i + j
            g = [
                [grad[zo * 64 : zo * 64 + 64, j * 256 + p * 128 : j * 256 + p * 128 + 128] for p in range(2)]
                for zo in range(2)
            ]
            cb = pltpu.roll(g[0][0], 64, 1)
            ab = g[1][0] + jnp.where(is_low, g[0][1], cb)
            c_low = cb + pltpu.roll(g[1][1], 64, 1)
            t = 3 * k // 2
            if k % 2 == 0:
                column(t, ab)
                held_a = c_low
            else:
                ba = pltpu.roll(ab, 64, 1)
                column(t, jnp.where(is_low, held_a, ba))
                column(t + 1, jnp.where(is_low, ba, pltpu.roll(c_low, 64, 1)))
    column(13, jnp.where(is_low, held_a, 0.0))
    first = send(sums.at[1 - core], half_in, other)

    firsts = []
    scatter = []
    for half in range(2):
        d_act = None
        for i in range(3):
            term = dot(rows_of(wide_del, half, i), back[i])
            d_act = term if d_act is None else d_act + term
        d_first = (d_act * slope_one[:, half * 256 : half * 256 + 256]).astype(BF16).astype(F32)
        scaled = (d_first.reshape(64, 8, 256) * times.reshape(1, 8, 1)).reshape(512, 256)
        high = scaled.astype(BF16)
        low = (scaled - high.astype(F32)).astype(BF16)
        firsts.append((high.T, low.T))
        if half == 0:
            first.wait_recv()
            half_sum[...] = sums[core] + half_in[...]
            for s, (dy, dx) in enumerate(steps):
                to, device = plane(dy, dx)
                scatter.append(
                    send(half_sum.at[pl.ds(pl.multiple_of(to * 32, 32), 32)], chunk_in.at[s], device)
                )
    lhs = jnp.concatenate([firsts[0][0], firsts[1][0], firsts[0][1], firsts[1][1]], axis=0)
    packed = jnp.zeros((64, 128), F32)
    for i in range(3):
        grad = dot(lhs, first_in[i : i + 8].reshape(512, 128))
        grad = grad[:512] + grad[512:]
        summed = None
        for zo in range(8):
            part = grad[zo * 64 : zo * 64 + 64]
            shift = (-3 * (zo - 1)) % 128
            part = pltpu.roll(part, shift, 1) if shift else part
            summed = part if summed is None else summed + part
        for j in range(3):
            start = 9 * (3 * i + j)
            shift = (start - 32 * j) % 128
            moved = pltpu.roll(summed, shift, 1) if shift else summed
            packed = jnp.where((lane >= start) & (lane < start + 9), moved, packed)
    first_sums[...] = packed

    own32 = pl.ds(pl.multiple_of(core * 32, 32), 32)
    f_first = send(
        first_sums.at[pl.ds(pl.multiple_of((1 - core) * 32, 32), 32)], f_in, other
    )
    ext[0:3, 2:18, 8:24, :] = vel[...]
    f_first.wait_recv()
    mine = first_sums[own32, :] + f_in[...]
    f_sum[...] = mine
    f_plane[spot] = mine
    f_across = [send(f_sum, f_plane.at[spot], plane(dy, dx)[1]) for dy, dx in steps]

    for part in scatter:
        part.wait_recv()
    mine = half_sum[pl.ds(pl.multiple_of(spot * 32, 32), 32), :]
    for s in range(15):
        mine = mine + chunk_in[s]
    chunk_sum[...] = mine
    deep_in[depth] = mine
    deep = [send(chunk_sum, deep_in.at[depth], device) for device in deeper]

    for rim in rims:
        rim.wait_recv()
    for c in range(4):
        for h in range(1 if c == 3 else 2):
            for i in range(16):
                to = 7 if c == 3 else 6 + h
                ext[c, 2 + i, to : to + 1, :] = y_in[0, 2 * c + h, i : i + 1, :]
                ext[c, 2 + i, 24 + h : 25 + h, :] = y_in[1, 2 * c + h, i : i + 1, :]

    def row(i, carry):
        def beside(c, here, far):
            turn = (254 - 4 * (base_of[c] + i)) % 128
            edge = pltpu.roll(z_in[slot_of[c]], turn, 1)
            out = []
            for m in (1, 2) if far else (1,):
                after = jnp.where(lane16 < m, edge, here)
                before = jnp.where(lane16 >= 128 - m, edge, here)
                out += [pltpu.roll(after, 128 - m, 1), pltpu.roll(before, m, 1)]
            return out

        centre = ext[3, 2 + i, 8:24, :]
        sides = [
            (ext[3, 3 + i, 8:24, :], ext[3, 1 + i, 8:24, :]),
            (ext[3, 2 + i, 9:25, :], ext[3, 2 + i, 7:23, :]),
            beside(3, centre, False),
        ]
        sides = [(0.5 * (centre + a), 0.5 * (centre + b)) for a, b in sides]
        speed = [ext[c, 2 + i, 8:24, :] for c in range(3)]
        for c in range(3):
            here = speed[c]
            near = [
                [ext[c, 2 + i + m, 8:24, :] for m in (1, -1, 2, -2)],
                [ext[c, 2 + i, 8 + m : 24 + m, :] for m in (1, -1, 2, -2)],
                beside(c, here, True),
            ]
            change = None
            for axis in range(3):
                a1, b1, a2, b2 = near[axis]
                slope = (8.0 * (a1 - b1) - (a2 - b2)) * (1.0 / 12.0)
                term = sides[axis][0] * (a1 - here) - sides[axis][1] * (here - b1)
                term = term - speed[axis] * slope
                change = term if change is None else change + term
            u_next[c, i] = here + 0.2 * change
        return carry

    lax.fori_loop(0, 16, row, 0)
    moves = [hand_over(0)]

    for part in f_across:
        part.wait_recv()
    mine = f_plane[0]
    for s in range(1, 16):
        mine = mine + f_plane[s]
    f_mid[...] = mine
    f_deep[depth] = mine
    f_planes = [send(f_mid, f_deep.at[depth], device) for device in deeper]

    for part in deep:
        part.wait_recv()
    mine = deep_in[0]
    for d in range(1, 8):
        mine = mine + deep_in[d]
    own = pl.ds(pl.multiple_of(spot * 32, 32), 32)
    total[core, own, :] = mine
    gather = [
        send(total.at[core, own], total.at[core, own], plane(dy, dx)[1]) for dy, dx in steps
    ]

    for part in f_planes:
        part.wait_recv()
    mine = f_deep[0]
    for d in range(1, 8):
        mine = mine + f_deep[d]
    f_total[own32, :] = mine
    f_last = send(f_total.at[own32], f_total.at[own32], other)

    across = []
    for dy in range(4):
        for part, (sy, _) in zip(gather, steps):
            if sy == dy:
                part.wait_recv()
        rows = pl.ds(pl.multiple_of(((y + 4 - dy) % 4) * 128, 128), 128)
        across.append(send(total.at[core, rows], total.at[core, rows], other))
    f_last.wait_recv()
    grad_first[...] = f_total[:, :81]
    moves.append(hand_over(2))
    for part in across:
        part.wait_recv()

    for t in range(14):
        wide = 64 if t == 13 else 128
        grad_hidden[:, t * 128 : t * 128 + wide] = total[t // 7, (t % 7) * 64 : (t % 7) * 64 + 64, :wide]
    grad_last[...] = total[1, 448:449, :64]
    losses = total[0, 448:464, :]
    at = lax.broadcasted_iota(jnp.int32, (16, 128), 0)
    losses = jnp.where(at == (gy * 2 + role) * 2 + gx // 16, losses, 0.0)
    losses = jnp.sum(losses, axis=0, keepdims=True)
    losses = pltpu.roll(losses, (128 - (gx % 16) * 8) % 128, 1)
    slot_loss[0] = losses[:, :8]
    moves += [hand_over(n) for n in (3, 4, 1)]
    for part in started:
        part.wait_send()
    for move in moves:
        move.wait()


SENDS = 7 + 1 + 15 + 1 + 15 + 7 + 7 + 15 + 1 + 4


def out_shapes():
    return (
        jax.ShapeDtypeStruct((3, 16, 16, 128), F32),
        jax.ShapeDtypeStruct((1, 1, 8), F32),
        jax.ShapeDtypeStruct((64, 81), F32),
        jax.ShapeDtypeStruct((64, 1728), F32),
        jax.ShapeDtypeStruct((1, 64), F32),
    )


def hand_out(*refs):
    sources, results, held, sems = refs[:5], refs[5:10], refs[10:15], refs[15]
    loads = [pltpu.make_async_copy(sources[n], held[n], sems.at[0, n]) for n in range(5)]
    stores = [pltpu.make_async_copy(held[n], results[n], sems.at[1, n]) for n in range(5)]
    order = (0, 3, 2, 1, 4)
    for n in order:
        loads[n].start()
    for n in order:
        loads[n].wait()
        stores[n].start()
    for n in order:
        stores[n].wait()


def on_device(velocity, target_visc, w_first, w_hidden, w_last, sample_owner, sample_block):
    anywhere = pl.BlockSpec(memory_space=pl.ANY)
    spread = spread_matrix()
    rows = (pool_matrix(), target_matrix(), spread[:, :256], spread[:, 256:], spread[:8, :256])
    consts = [jnp.asarray(np.concatenate(rows, 0)), jnp.asarray(first_selector())]
    args = [
        velocity, target_visc, w_first, w_hidden, w_last.reshape(1, 64),
        sample_owner.reshape(1, 256), sample_block.reshape(1, 256), *consts,
    ]
    outs = pl.pallas_call(
        whole_kernel,
        out_shape=out_shapes(),
        in_specs=[anywhere] * 9,
        out_specs=(anywhere,) * 5,
        scratch_shapes=[pltpu.VMEM(a.shape, a.dtype) for a in args + list(out_shapes())] + [
            pltpu.VMEM((512, 128), F32),
            pltpu.VMEM((10, 64, 128), BF16),
            pltpu.VMEM((3, 512, 128), BF16),
            pltpu.VMEM((3, 256, 1152), BF16),
            pltpu.VMEM((3, 1152, 256), BF16),
            pltpu.VMEM((2, 10, 64, 1152), BF16),
            pltpu.VMEM((2, 10, 64, 1152), BF16),
            pltpu.VMEM((512, 512), F32),
            pltpu.VMEM((4, 10, 64, 768), BF16),
            pltpu.VMEM((2, 512, 128), F32),
            pltpu.VMEM((2, 512, 128), F32),
            pltpu.VMEM((64, 128), F32),
            pltpu.VMEM((4, 20, 32, 128), F32),
            pltpu.VMEM((2, 7, 16, 128), F32),
            pltpu.VMEM((2, 7, 16, 128), F32),
            pltpu.VMEM((3, 16, 128), F32),
            pltpu.VMEM((3, 16, 128), F32),
            pltpu.VMEM((512, 128), F32),
            pltpu.VMEM((512, 128), F32),
            pltpu.VMEM((15, 32, 128), F32),
            pltpu.VMEM((32, 128), F32),
            pltpu.VMEM((8, 32, 128), F32),
            pltpu.VMEM((2, 512, 128), F32),
            pltpu.VMEM((32, 128), F32),
            pltpu.VMEM((32, 128), F32),
            pltpu.VMEM((16, 32, 128), F32),
            pltpu.VMEM((32, 128), F32),
            pltpu.VMEM((8, 32, 128), F32),
            pltpu.VMEM((64, 128), F32),
            pltpu.SemaphoreType.DMA((14,)),
            pltpu.SemaphoreType.DMA((2, SENDS)),
        ],
        compiler_params=pltpu.CompilerParams(
            vmem_limit_bytes=60 * 1024 * 1024, collective_id=0, has_side_effects=True
        ),
        name="whole",
    )(*args)
    outs = pl.pallas_call(
        hand_out,
        out_shape=out_shapes(),
        in_specs=[anywhere] * 5,
        out_specs=(anywhere,) * 5,
        scratch_shapes=[pltpu.VMEM(a.shape, a.dtype) for a in out_shapes()]
        + [pltpu.SemaphoreType.DMA((2, 5))],
        compiler_params=pltpu.CompilerParams(vmem_limit_bytes=60 * 1024 * 1024),
        name="hand_out",
    )(*outs)
    u_next, slot_loss, grad_first, grad_hidden, grad_last = outs
    return (u_next, slot_loss, grad_first, grad_hidden, grad_last.reshape(64))


def solution(mesh):
    return jax.shard_map(
        on_device,
        mesh=mesh,
        in_specs=(
            P(None, "gx", "gy", "role"),
            P("gx", "gy", "role"),
            P(),
            P(),
            P(),
            P("gy", "role", None, None),
            P("gy", "role", None, None),
        ),
        out_specs=(P(None, "gx", "gy", "role"), P("gy", "role", "gx"), P(), P(), P()),
        check_vma=False,
    )
```

```python
import numpy as np
import jax
import jax.numpy as jnp
from jax import lax
from jax.sharding import PartitionSpec as P
from jax.experimental import pallas as pl
from jax.experimental.pallas import tpu as pltpu

SIDE = 8
CH = 64
F32 = jnp.float32
BF16 = jnp.bfloat16
NT = (((1,), (1,)), ((), ()))
NN = (((1,), (0,)), ((), ()))
MESH = pl.DeviceIdType.MESH


def dot(a, b, dims=NN):
    return lax.dot_general(a, b, dims, preferred_element_type=F32)


def pool_matrix():
    z = np.arange(128)[:, None]
    lane = np.arange(256)[None, :]
    block, inner = lane // 32, lane % 32
    parts = []
    for comp in range(3):
        hit = (inner < 24) & (inner % 3 == comp) & (z // 2 == block * 8 + inner // 3)
        parts.append(np.where(hit, 0.125, 0.0))
    return np.concatenate(parts, 0).astype(jnp.bfloat16)


def target_matrix():
    z = np.arange(64)[:, None]
    lane = np.arange(256)[None, :]
    block, inner = lane // 32, lane % 32
    return ((inner >= 24) & (z == block * 8 + inner - 24)).astype(jnp.bfloat16)


def spread_matrix():
    row = np.arange(128)[:, None]
    lane = np.arange(256)[None, :]
    return (row == 24 + lane // 128 * 4 + lane // 2 % 4).astype(jnp.bfloat16)


def first_selector():
    out = np.zeros((81, 3, 8, 128), np.float32)
    for i in range(3):
        for zo in range(8):
            for j in range(3):
                for t in range(9):
                    zi = zo - 1 + t // 3
                    if 0 <= zi < 8:
                        out[9 * (3 * i + j) + t, i, zo, j * 32 + zi * 3 + t % 3] = 1.0
    return out.reshape(81, 3072).astype(jnp.bfloat16)


def lane_of(shape):
    return lax.broadcasted_iota(jnp.int32, shape, len(shape) - 1)


def shift_y(field, shift):
    zero = jnp.zeros((8, 8, field.shape[2]), field.dtype)
    if shift < 0:
        return jnp.concatenate([zero, field[:, :56]], axis=1)
    if shift > 0:
        return jnp.concatenate([field[:, 8:], zero], axis=1)
    return field


def widen(store, field):
    low = lane_of((8, 64, 128)) < 64
    zero = jnp.zeros((64, 960), BF16)
    for half in range(2):
        store[half, 0] = zero
        store[half, 9] = zero
        main = field[:, half * 256 : half * 256 + 256].reshape(8, 64, 256)
        next_z = field[:, 256:384] if half == 0 else field[:, 128:256]
        turned = pltpu.roll(next_z, 64, 1).reshape(8, 64, 128)
        next_z = next_z.reshape(8, 64, 128)
        in_low, in_high = (next_z, turned) if half == 0 else (turned, next_z)
        for j in range(3):
            store[half, 1:9, :, j * 256 : (j + 1) * 256] = shift_y(main, j - 1).astype(BF16)
        edge = jnp.where(low, shift_y(in_low, -1), in_high)
        store[half, 1:9, :, 768:896] = edge.astype(BF16)
        store[half, 1:9, :, 896:960] = shift_y(in_low, 1)[:, :, :64].astype(BF16)


def widen_pairs(store, field):
    low = lane_of((512, 128)) < 64
    zero = jnp.zeros((64, 768), BF16)
    none = jnp.zeros((512, 128), F32)
    pairs = [field[:, p * 128 : (p + 1) * 128] for p in range(4)]
    turned = [none] + [pltpu.roll(p, 64, 1) for p in pairs] + [none]
    for p in range(4):
        store[p, 0] = zero
        store[p, 9] = zero
        near = jnp.where(low, turned[p], turned[p + 2])
        whole = jnp.concatenate([pairs[p], near], axis=1).reshape(8, 64, 256)
        for j in range(3):
            store[p, 1:9, :, j * 256 : (j + 1) * 256] = shift_y(whole, j - 1).astype(BF16)


def rows_of(store, half, i):
    return store[half, i : i + 8].reshape(512, 960)


def place_weights(w_hidden, ahead, back):
    lane = lane_of((64, 128))
    low = lane < 64
    zero = jnp.zeros((64, 128), BF16)
    tiles = [w_hidden[:, t * 128 : (t + 1) * 128] for t in range(13)]
    last = w_hidden[:, 1664:1728]
    tiles.append(jnp.concatenate([last, last], axis=1))
    tiles = [t.astype(F32) for t in tiles]
    swapped = [pltpu.roll(t, 64, 1) for t in tiles]
    lows, highs = [], []
    for j in range(9):
        t = 3 * j // 2
        if j % 2 == 0:
            ab = tiles[t]
            bc = jnp.where(low, swapped[t], swapped[t + 1])
            c_low, c_high = tiles[t + 1], swapped[t + 1]
            a_low, a_high = tiles[t], swapped[t]
        else:
            bc = tiles[t + 1]
            ab = jnp.where(low, swapped[t], swapped[t + 1])
            c_low, c_high = swapped[t + 1], tiles[t + 1]
            a_low, a_high = swapped[t], tiles[t]
        lows.append((c_low, a_low))
        highs.append((c_high, a_high))
        c_0 = jnp.where(low, c_low, 0.0).astype(BF16)
        o_a = jnp.where(low, 0.0, a_high).astype(BF16)
        ab = ab.astype(BF16)
        bc = bc.astype(BF16)
        rows = [(bc, zero), (ab, c_0), (o_a, bc), (zero, ab)]
        flip = 8 - j
        for half in range(2):
            for z in range(4):
                at = slice(z * 64, (z + 1) * 64)
                for part in range(2):
                    start = (j % 3) * 256 + part * 128
                    ahead[half, j // 3, at, start : start + 128] = rows[z][part]
                    start = (flip % 3) * 256 + z * 64
                    cut = slice(part * 128, (part + 1) * 128)
                    back[half, flip // 3, start : start + 64, cut] = rows[z][part]
        start = 768 + (flip % 3) * 64
        back[0, flip // 3, start : start + 64, 0:128] = zero
        back[0, flip // 3, start : start + 64, 128:256] = o_a
        back[1, flip // 3, start : start + 64, 0:128] = c_0
        back[1, flip // 3, start : start + 64, 128:256] = zero
    for half in range(2):
        for i in range(3):
            edge = jnp.where(low, lows[3 * i][half], highs[3 * i + 1][half]).astype(BF16)
            end = lows[3 * i + 2][half][:, :64].astype(BF16)
            for z in range(4):
                at = slice(z * 64, (z + 1) * 64)
                here = z == (3 if half == 0 else 0)
                ahead[half, i, at, 768:896] = edge if here else zero
                ahead[half, i, at, 896:960] = end if here else zero[:, :64]


def whole_kernel(*refs):
    sources, refs = refs[:9], refs[9:]
    (u_result, f_result, result), refs = refs[:3], refs[3:]
    held_in, refs = refs[:9], refs[9:]
    vel, target, w_first, w_hidden, w_last, owner, block, fixed, sel = held_in
    (
        u_next,
        filt, first_in, w_one, ahead, back, wide_act, wide_del, slope_one, pair_act, eddy_z,
        sums, first_sums, ext, y_out, y_in, z_out, z_in,
        half_in, half_sum, chunk_in, chunk_sum, deep_in, total,
        f_in, f_sum, f_plane, f_mid, f_deep, f_total,
        local_sems, sems,
    ) = refs

    loads = [
        pltpu.make_async_copy(src, dst, local_sems.at[n])
        for n, (src, dst) in enumerate(zip(sources, held_in))
    ]
    for n in (3, 0, 2, 8, 7, 1, 4, 5, 6):
        loads[n].start()

    moves = []

    def hand_over(src, dst):
        moves.append(pltpu.make_async_copy(src, dst, local_sems.at[9 + len(moves)]))
        moves[-1].start()

    gx, gy, role = lax.axis_index("gx"), lax.axis_index("gy"), lax.axis_index("role")
    depth, y = gx // 4, gx % 4
    x, core = (gy // 2) * 2 + role, gy % 2
    spot = y * 4 + x

    def plane(dy, dx):
        to_y, to_x = (y + dy) % 4, (x + dx) % 4
        return to_y * 4 + to_x, (depth * 4 + to_y, (to_x // 2) * 2 + core, to_x % 2)

    reach = (0, 1, 2, 1)
    steps = [(dy, dx) for dy in range(4) for dx in range(4) if dy or dx]
    steps.sort(key=lambda s: -reach[s[0]] - reach[s[1]])
    deeper = [(((depth + d) % 8) * 4 + y, gy, role) for d in (4, 3, 5, 2, 6, 1, 7)]
    other = (gx, gy - core + 1 - core, role)
    x_up, x_down = ((gx + 1) % 32, gy, role), ((gx + 31) % 32, gy, role)
    y_up, y_down = (gx, (gy + 1) % 4, role), (gx, (gy + 3) % 4, role)
    z_side = (gx, gy, 1 - role)

    barrier = pltpu.get_barrier_semaphore()
    greeted = [plane(dy, dx)[1] for dy, dx in steps] + deeper + [x_up, x_down, y_up, y_down]
    for device in greeted:
        pl.semaphore_signal(barrier, inc=1, device_id=device, device_id_type=MESH)

    started = []

    def send(src, dst, device):
        at = len(started)
        part = pltpu.make_async_remote_copy(
            src_ref=src, dst_ref=dst, send_sem=sems.at[0, at], recv_sem=sems.at[1, at],
            device_id=device, device_id_type=MESH,
        )
        started.append(part)
        part.start()
        return part

    for n in (3, 0, 2, 8, 7, 1, 4, 5, 6):
        loads[n].wait()
    place_weights(w_hidden, ahead, back)
    placed = dot(w_first[...], sel[...]).astype(BF16)
    for i in range(3):
        for zo in range(8):
            at = (i * 8 + zo) * 128
            w_one[i, zo * 64 : (zo + 1) * 64, :] = placed[:, at : at + 128]

    pooled = []
    for comp in range(3):
        summed = None
        for dx in range(2):
            for dy in range(2):
                part = jnp.concatenate(
                    [vel[comp, 2 * i + dx, pl.ds(dy, 8, stride=2), :] for i in range(8)], axis=0
                )
                summed = part if summed is None else summed + part
        pooled.append(summed)
    rest = jnp.concatenate(pooled, axis=1)
    blocks = None
    for _ in range(3):
        piece = rest.astype(BF16)
        rest = rest - piece.astype(F32)
        term = dot(piece, fixed[0:384])
        blocks = term if blocks is None else blocks + term
    blocks = blocks.astype(BF16).astype(F32)
    want = target[...].astype(F32).reshape(64, 64).astype(BF16)
    blocks = blocks + dot(want, fixed[384:448])
    for b in range(8):
        tile = blocks[:, (b // 4) * 128 : (b // 4) * 128 + 128]
        if b % 4:
            tile = pltpu.roll(tile, 128 - 32 * (b % 4), 1)
        filt[pl.ds(b, 64, stride=8), :] = tile
    held = filt[...]
    targets = dot(held.astype(BF16), fixed[448:576])
    lane = lane_of((512, 128))
    inputs = jnp.where(lane < 24, held, 0.0).reshape(8, 64, 128)
    near = shift_y(inputs, -1)
    near = near + pltpu.roll(inputs.reshape(512, 128), 32, 1).reshape(8, 64, 128)
    near = near + pltpu.roll(shift_y(inputs, 1).reshape(512, 128), 64, 1).reshape(8, 64, 128)
    first_in[0] = jnp.zeros((64, 128), BF16)
    first_in[9] = jnp.zeros((64, 128), BF16)
    first_in[1:9] = near.astype(BF16)

    pre = None
    for i in range(3):
        term = dot(first_in[i : i + 8].reshape(512, 128), w_one[i], NT)
        pre = term if pre is None else pre + term
    sig = 1.0 / (1.0 + jnp.exp(-pre))
    slope_one[...] = sig * (1.0 + pre * (1.0 - sig))
    acts = (pre * sig).astype(BF16).astype(F32)
    widen(wide_act, acts)
    widen_pairs(pair_act, acts)

    slot_of, base_of = (0, 0, 1, 2), (0, 16, 0, 0)
    lane16 = lane_of((16, 128))

    def pack_sides(c, field, wide):
        for h in range(wide):
            for i in range(16):
                low, high = field[i, h : h + 1, :], field[i, 16 - wide + h : 17 - wide + h, :]
                y_out[0, 2 * c + h, i : i + 1, :] = low
                y_out[1, 2 * c + h, i : i + 1, :] = high
        packed = None
        for i in range(16):
            g = base_of[c] + i
            moved = pltpu.roll(field[i], 2 + 4 * g, 1)
            packed = moved if packed is None else jnp.where(lane16 // 4 == g, moved, packed)
        return packed

    sides_of = [pack_sides(c, vel.at[c], 2) for c in range(3)]
    z_out[0] = jnp.where(lane16 < 64, sides_of[0], sides_of[1])
    z_out[1] = sides_of[2]

    wl = w_last[...].astype(F32)
    wl = jnp.concatenate([wl, wl, wl, wl], axis=1)
    rows_iota = lax.broadcasted_iota(jnp.int32, (128, 256), 0)
    lanes_iota = lax.broadcasted_iota(jnp.int32, (128, 256), 1)
    out_map = jnp.where(rows_iota // 2 % 4 == lanes_iota // 64, wl, 0.0).astype(BF16)
    repeat = jnp.where(rows_iota == lanes_iota // 64 * 2, 1.0, 0.0).astype(BF16)

    number = lax.broadcasted_iota(jnp.int32, (8, 256), 0)
    drawn = jnp.where((owner[...] == gx) & (block[...] == number), 1.0, 0.0)
    times = jnp.sum(drawn, axis=1, keepdims=True)

    loss = jnp.zeros((8, 128), F32)
    last = jnp.zeros((8, 256), F32)
    deltas, parts = [], []
    for half in range(2):
        pre = None
        for i in range(3):
            term = dot(rows_of(wide_act, half, i), ahead[half, i], NT)
            pre = term if pre is None else pre + term
        sig = 1.0 / (1.0 + jnp.exp(-pre))
        act = (pre * sig).astype(BF16)
        slope = sig * (1.0 + pre * (1.0 - sig))
        logits = dot(act, out_map, NT)
        small = jnp.exp(-jnp.abs(logits))
        eddy = 0.5 * (jnp.maximum(logits, 0.0) + jnp.log1p(small))
        eddy_z[half] = eddy
        gate = jnp.where(logits >= 0, 1.0, small) / (1.0 + small)
        error = eddy - targets[:, half * 128 : half * 128 + 128]
        loss = loss + jnp.sum((error * error).reshape(64, 8, 128), axis=0)
        d_logit = dot((error * gate * (1.0 / (256 * 512))).astype(BF16), repeat)
        last = last + jnp.sum((d_logit * act.astype(F32)).reshape(64, 8, 256), axis=0)
        delta = (wl * d_logit * slope).astype(BF16).astype(F32)
        deltas.append(delta)
        scaled = (delta.reshape(64, 8, 256) * times.reshape(1, 8, 1)).reshape(512, 256)
        high = scaled.astype(BF16)
        low = (scaled - high.astype(F32)).astype(BF16)
        for p in range(2):
            cut = slice(p * 128, p * 128 + 128)
            parts.append(jnp.concatenate([high[:, cut].T, low[:, cut].T], axis=0))
    widen(wide_del, jnp.concatenate(deltas, axis=1))

    lane = lane_of((64, 128))
    field = jnp.zeros((64, 128), F32)
    for half in range(2):
        for b in range(8):
            part = eddy_z[half, pl.ds(b, 64, stride=8), :]
            field = jnp.where(lane // 8 == 2 * b + half, part, field)
    field = 0.02 + field
    for i in range(8):
        for dx in range(2):
            for dy in range(2):
                ext[3, 2 + 2 * i + dx, pl.ds(8 + dy, 8, stride=2), :] = field[i * 8 : i * 8 + 8]
    z_out[2] = pack_sides(3, ext.at[3, 2:18, 8:24], 1)
    pl.semaphore_wait(barrier, len(greeted))
    rims = [
        send(vel.at[:, 0:2], ext.at[0:3, 18:20, 8:24], x_down),
        send(vel.at[:, 14:16], ext.at[0:3, 0:2, 8:24], x_up),
        send(ext.at[3, 2:3, 8:24], ext.at[3, 18:19, 8:24], x_down),
        send(ext.at[3, 17:18, 8:24], ext.at[3, 1:2, 8:24], x_up),
        send(y_out.at[0], y_in.at[1], y_down),
        send(y_out.at[1], y_in.at[0], y_up),
        send(z_out, z_in, z_side),
    ]

    per_block = jnp.sum(loss, axis=1, keepdims=True) * (1.0 / (32 * 512))
    by_slot = jnp.sum(drawn * per_block, axis=0, keepdims=True)
    group = gy * 2 + role
    at = lax.broadcasted_iota(jnp.int32, (64, 128), 0)
    by_slot = jnp.where(at % 2 == 0, by_slot[:, :128], by_slot[:, 128:])
    sums[0, 448:512, :] = jnp.where(at // 2 == group, by_slot, 0.0)
    last = jnp.sum(last * times, axis=0, keepdims=True)
    last = last[:, :128] + last[:, 128:]
    last = last + pltpu.roll(last, 64, 1)
    sums[1, 448:512, :] = jnp.broadcast_to(last, (64, 128))

    def column(t, value):
        sums[t // 7, (t % 7) * 64 : (t % 7) * 64 + 64, :] = value

    is_low = lane < 64
    held_a = None
    for i in range(3):
        grad = None
        for p in range(4):
            term = dot(parts[p], pair_act[p, i : i + 8].reshape(512, 768))
            grad = term if grad is None else grad + term
        grad = grad[:128] + grad[128:]
        for j in range(3):
            k = 3 * i + j
            g = [
                [grad[zo * 64 : zo * 64 + 64, j * 256 + p * 128 : j * 256 + p * 128 + 128] for p in range(2)]
                for zo in range(2)
            ]
            cb = pltpu.roll(g[0][0], 64, 1)
            ab = g[1][0] + jnp.where(is_low, g[0][1], cb)
            c_low = cb + pltpu.roll(g[1][1], 64, 1)
            t = 3 * k // 2
            if k % 2 == 0:
                column(t, ab)
                held_a = c_low
            else:
                ba = pltpu.roll(ab, 64, 1)
                column(t, jnp.where(is_low, held_a, ba))
                column(t + 1, jnp.where(is_low, ba, pltpu.roll(c_low, 64, 1)))
    column(13, jnp.where(is_low, held_a, 0.0))
    first = send(sums.at[1 - core], half_in, other)

    firsts = []
    scatter = []
    for half in range(2):
        d_act = None
        for i in range(3):
            term = dot(rows_of(wide_del, half, i), back[half, i])
            d_act = term if d_act is None else d_act + term
        d_first = (d_act * slope_one[:, half * 256 : half * 256 + 256]).astype(BF16).astype(F32)
        scaled = (d_first.reshape(64, 8, 256) * times.reshape(1, 8, 1)).reshape(512, 256)
        high = scaled.astype(BF16)
        low = (scaled - high.astype(F32)).astype(BF16)
        firsts.append((high.T, low.T))
        if half == 0:
            first.wait_recv()
            half_sum[...] = sums[core] + half_in[...]
            for s, (dy, dx) in enumerate(steps):
                to, device = plane(dy, dx)
                scatter.append(
                    send(half_sum.at[pl.ds(pl.multiple_of(to * 32, 32), 32)], chunk_in.at[s], device)
                )
    lhs = jnp.concatenate([firsts[0][0], firsts[1][0], firsts[0][1], firsts[1][1]], axis=0)
    packed = jnp.zeros((64, 128), F32)
    for i in range(3):
        grad = dot(lhs, first_in[i : i + 8].reshape(512, 128))
        grad = grad[:512] + grad[512:]
        summed = None
        for zo in range(8):
            part = grad[zo * 64 : zo * 64 + 64]
            shift = (-3 * (zo - 1)) % 128
            part = pltpu.roll(part, shift, 1) if shift else part
            summed = part if summed is None else summed + part
        for j in range(3):
            start = 9 * (3 * i + j)
            shift = (start - 32 * j) % 128
            moved = pltpu.roll(summed, shift, 1) if shift else summed
            packed = jnp.where((lane >= start) & (lane < start + 9), moved, packed)
    first_sums[...] = packed

    own32 = pl.ds(pl.multiple_of(core * 32, 32), 32)
    f_first = send(
        first_sums.at[pl.ds(pl.multiple_of((1 - core) * 32, 32), 32)], f_in, other
    )
    ext[0:3, 2:18, 8:24, :] = vel[...]
    f_first.wait_recv()
    mine = first_sums[own32, :] + f_in[...]
    f_sum[...] = mine
    f_plane[spot] = mine
    f_across = [send(f_sum, f_plane.at[spot], plane(dy, dx)[1]) for dy, dx in steps]

    for part in scatter:
        part.wait_recv()
    mine = half_sum[pl.ds(pl.multiple_of(spot * 32, 32), 32), :]
    for s in range(15):
        mine = mine + chunk_in[s]
    chunk_sum[...] = mine
    deep_in[depth] = mine
    deep = [send(chunk_sum, deep_in.at[depth], device) for device in deeper]

    for rim in rims:
        rim.wait_recv()
    for c in range(4):
        for h in range(1 if c == 3 else 2):
            for i in range(16):
                to = 7 if c == 3 else 6 + h
                ext[c, 2 + i, to : to + 1, :] = y_in[0, 2 * c + h, i : i + 1, :]
                ext[c, 2 + i, 24 + h : 25 + h, :] = y_in[1, 2 * c + h, i : i + 1, :]

    def row(i, carry):
        def beside(c, here, far):
            turn = (254 - 4 * (base_of[c] + i)) % 128
            edge = pltpu.roll(z_in[slot_of[c]], turn, 1)
            out = []
            for m in (1, 2) if far else (1,):
                after = jnp.where(lane16 < m, edge, here)
                before = jnp.where(lane16 >= 128 - m, edge, here)
                out += [pltpu.roll(after, 128 - m, 1), pltpu.roll(before, m, 1)]
            return out

        centre = ext[3, 2 + i, 8:24, :]
        sides = [
            (ext[3, 3 + i, 8:24, :], ext[3, 1 + i, 8:24, :]),
            (ext[3, 2 + i, 9:25, :], ext[3, 2 + i, 7:23, :]),
            beside(3, centre, False),
        ]
        sides = [(0.5 * (centre + a), 0.5 * (centre + b)) for a, b in sides]
        speed = [ext[c, 2 + i, 8:24, :] for c in range(3)]
        for c in range(3):
            here = speed[c]
            near = [
                [ext[c, 2 + i + m, 8:24, :] for m in (1, -1, 2, -2)],
                [ext[c, 2 + i, 8 + m : 24 + m, :] for m in (1, -1, 2, -2)],
                beside(c, here, True),
            ]
            change = None
            for axis in range(3):
                a1, b1, a2, b2 = near[axis]
                slope = (8.0 * (a1 - b1) - (a2 - b2)) * (1.0 / 12.0)
                term = sides[axis][0] * (a1 - here) - sides[axis][1] * (here - b1)
                term = term - speed[axis] * slope
                change = term if change is None else change + term
            u_next[c, i] = here + 0.2 * change
        return carry

    lax.fori_loop(0, 16, row, 0)
    hand_over(u_next, u_result)

    for part in f_across:
        part.wait_recv()
    mine = f_plane[0]
    for s in range(1, 16):
        mine = mine + f_plane[s]
    f_mid[...] = mine
    f_deep[depth] = mine
    f_planes = [send(f_mid, f_deep.at[depth], device) for device in deeper]

    for part in deep:
        part.wait_recv()
    mine = deep_in[0]
    for d in range(1, 8):
        mine = mine + deep_in[d]
    own = pl.ds(pl.multiple_of(spot * 32, 32), 32)
    total[core, own, :] = mine
    gather = [
        send(total.at[core, own], total.at[core, own], plane(dy, dx)[1]) for dy, dx in steps
    ]

    for part in f_planes:
        part.wait_recv()
    mine = f_deep[0]
    for d in range(1, 8):
        mine = mine + f_deep[d]
    f_total[own32, :] = mine
    f_last = send(f_total.at[own32], f_total.at[own32], other)

    across = []
    for dy in range(4):
        for part, (sy, _) in zip(gather, steps):
            if sy == dy:
                part.wait_recv()
        rows = pl.ds(pl.multiple_of(((y + 4 - dy) % 4) * 128, 128), 128)
        across.append(send(total.at[core, rows], result.at[core, rows], other))
    hand_over(total.at[core], result.at[core])
    f_last.wait_recv()
    hand_over(f_total, f_result)
    for part in across:
        part.wait_recv()
    for part in started:
        part.wait_send()
    for move in moves:
        move.wait()


SENDS = 7 + 1 + 15 + 1 + 15 + 7 + 7 + 15 + 1 + 4


def out_shapes():
    return (
        jax.ShapeDtypeStruct((3, 16, 16, 128), F32),
        jax.ShapeDtypeStruct((1, 1, 8), F32),
        jax.ShapeDtypeStruct((64, 81), F32),
        jax.ShapeDtypeStruct((64, 1728), F32),
        jax.ShapeDtypeStruct((1, 64), F32),
    )


def hand_out(
    u_source, f_source, source, u_result, loss_result, first_result, hidden_result, last_result,
    u_held, f_held, held, slot_loss, grad_first, grad_hidden, grad_last, sems,
):
    gx, gy, role = lax.axis_index("gx"), lax.axis_index("gy"), lax.axis_index("role")
    loads = [
        pltpu.make_async_copy(source, held, sems.at[0]),
        pltpu.make_async_copy(u_source, u_held, sems.at[1]),
        pltpu.make_async_copy(f_source, f_held, sems.at[2]),
    ]
    stores = [
        pltpu.make_async_copy(grad_hidden, hidden_result, sems.at[3]),
        pltpu.make_async_copy(u_held, u_result, sems.at[4]),
        pltpu.make_async_copy(grad_first, first_result, sems.at[5]),
        pltpu.make_async_copy(grad_last, last_result, sems.at[6]),
        pltpu.make_async_copy(slot_loss, loss_result, sems.at[7]),
    ]
    for load in loads:
        load.start()
    loads[0].wait()
    for t in range(14):
        wide = 64 if t == 13 else 128
        rows = slice((t % 7) * 64, (t % 7) * 64 + 64)
        grad_hidden[:, t * 128 : t * 128 + wide] = held[t // 7, rows, :wide]
    stores[0].start()
    loads[1].wait()
    stores[1].start()
    loads[2].wait()
    grad_first[...] = f_held[:, :81]
    grad_last[...] = held[1, 448:449, :64]
    losses = held[0, 448:464, :]
    at = lax.broadcasted_iota(jnp.int32, (16, 128), 0)
    losses = jnp.where(at == (gy * 2 + role) * 2 + gx // 16, losses, 0.0)
    losses = jnp.sum(losses, axis=0, keepdims=True)
    losses = pltpu.roll(losses, (128 - (gx % 16) * 8) % 128, 1)
    slot_loss[0] = losses[:, :8]
    for store in stores[2:]:
        store.start()
    for store in stores:
        store.wait()


def on_device(velocity, target_visc, w_first, w_hidden, w_last, sample_owner, sample_block):
    anywhere = pl.BlockSpec(memory_space=pl.ANY)
    spread = spread_matrix()
    rows = (pool_matrix(), target_matrix(), spread, spread[:8])
    consts = [jnp.asarray(np.concatenate(rows, 0)), jnp.asarray(first_selector())]
    args = [
        velocity, target_visc, w_first, w_hidden, w_last.reshape(1, 64),
        sample_owner.reshape(1, 256), sample_block.reshape(1, 256), *consts,
    ]
    sums = [
        jax.ShapeDtypeStruct(shape, F32) for shape in ((3, 16, 16, 128), (64, 128), (2, 512, 128))
    ]
    outs = pl.pallas_call(
        whole_kernel,
        out_shape=sums,
        in_specs=[anywhere] * 9,
        out_specs=(anywhere,) * 3,
        scratch_shapes=[pltpu.VMEM(a.shape, a.dtype) for a in args] + [
            pltpu.VMEM((3, 16, 16, 128), F32),
            pltpu.VMEM((512, 128), F32),
            pltpu.VMEM((10, 64, 128), BF16),
            pltpu.VMEM((3, 512, 128), BF16),
            pltpu.VMEM((2, 3, 256, 960), BF16),
            pltpu.VMEM((2, 3, 960, 256), BF16),
            pltpu.VMEM((2, 10, 64, 960), BF16),
            pltpu.VMEM((2, 10, 64, 960), BF16),
            pltpu.VMEM((512, 512), F32),
            pltpu.VMEM((4, 10, 64, 768), BF16),
            pltpu.VMEM((2, 512, 128), F32),
            pltpu.VMEM((2, 512, 128), F32),
            pltpu.VMEM((64, 128), F32),
            pltpu.VMEM((4, 20, 32, 128), F32),
            pltpu.VMEM((2, 7, 16, 128), F32),
            pltpu.VMEM((2, 7, 16, 128), F32),
            pltpu.VMEM((3, 16, 128), F32),
            pltpu.VMEM((3, 16, 128), F32),
            pltpu.VMEM((512, 128), F32),
            pltpu.VMEM((512, 128), F32),
            pltpu.VMEM((15, 32, 128), F32),
            pltpu.VMEM((32, 128), F32),
            pltpu.VMEM((8, 32, 128), F32),
            pltpu.VMEM((2, 512, 128), F32),
            pltpu.VMEM((32, 128), F32),
            pltpu.VMEM((32, 128), F32),
            pltpu.VMEM((16, 32, 128), F32),
            pltpu.VMEM((32, 128), F32),
            pltpu.VMEM((8, 32, 128), F32),
            pltpu.VMEM((64, 128), F32),
            pltpu.SemaphoreType.DMA((12,)),
            pltpu.SemaphoreType.DMA((2, SENDS)),
        ],
        compiler_params=pltpu.CompilerParams(
            vmem_limit_bytes=60 * 1024 * 1024, collective_id=0, has_side_effects=True
        ),
        name="whole",
    )(*args)
    outs = pl.pallas_call(
        hand_out,
        out_shape=out_shapes(),
        in_specs=[anywhere] * 3,
        out_specs=(anywhere,) * 5,
        scratch_shapes=[pltpu.VMEM(a.shape, a.dtype) for a in [*sums, *out_shapes()[1:]]]
        + [pltpu.SemaphoreType.DMA((8,))],
        compiler_params=pltpu.CompilerParams(vmem_limit_bytes=60 * 1024 * 1024),
        name="hand_out",
    )(*outs)
    u_next, slot_loss, grad_first, grad_hidden, grad_last = outs
    return (u_next, slot_loss, grad_first, grad_hidden, grad_last.reshape(64))


def solution(mesh):
    return jax.shard_map(
        on_device,
        mesh=mesh,
        in_specs=(
            P(None, "gx", "gy", "role"),
            P("gx", "gy", "role"),
            P(),
            P(),
            P(),
            P("gy", "role", None, None),
            P("gy", "role", None, None),
        ),
        out_specs=(P(None, "gx", "gy", "role"), P("gy", "role", "gx"), P(), P(), P()),
        check_vma=False,
    )
```

```python
import numpy as np
import jax
import jax.numpy as jnp
from jax import lax
from jax.sharding import PartitionSpec as P
from jax.experimental import pallas as pl
from jax.experimental.pallas import tpu as pltpu

SIDE = 8
CH = 64
F32 = jnp.float32
BF16 = jnp.bfloat16
NT = (((1,), (1,)), ((), ()))
NN = (((1,), (0,)), ((), ()))
MESH = pl.DeviceIdType.MESH


def dot(a, b, dims=NN):
    return lax.dot_general(a, b, dims, preferred_element_type=F32)


def pool_matrix():
    z = np.arange(128)[:, None]
    lane = np.arange(256)[None, :]
    block, inner = lane // 32, lane % 32
    parts = []
    for comp in range(3):
        hit = (inner < 24) & (inner % 3 == comp) & (z // 2 == block * 8 + inner // 3)
        parts.append(np.where(hit, 0.125, 0.0))
    return np.concatenate(parts, 0).astype(jnp.bfloat16)


def target_matrix():
    z = np.arange(64)[:, None]
    lane = np.arange(256)[None, :]
    block, inner = lane // 32, lane % 32
    return ((inner >= 24) & (z == block * 8 + inner - 24)).astype(jnp.bfloat16)


def spread_matrix():
    row = np.arange(128)[:, None]
    lane = np.arange(256)[None, :]
    return (row == 24 + lane // 128 * 4 + lane // 2 % 4).astype(jnp.bfloat16)


def first_selector():
    out = np.zeros((81, 3, 8, 128), np.float32)
    for i in range(3):
        for zo in range(8):
            for j in range(3):
                for t in range(9):
                    zi = zo - 1 + t // 3
                    if 0 <= zi < 8:
                        out[9 * (3 * i + j) + t, i, zo, j * 32 + zi * 3 + t % 3] = 1.0
    return out.reshape(81, 3072).astype(jnp.bfloat16)


def lane_of(shape):
    return lax.broadcasted_iota(jnp.int32, shape, len(shape) - 1)


def shift_y(field, shift):
    zero = jnp.zeros((8, 8, field.shape[2]), field.dtype)
    if shift < 0:
        return jnp.concatenate([zero, field[:, :56]], axis=1)
    if shift > 0:
        return jnp.concatenate([field[:, 8:], zero], axis=1)
    return field


def widen(store, field):
    low = lane_of((8, 64, 128)) < 64
    zero = jnp.zeros((64, 960), BF16)
    for half in range(2):
        store[half, 0] = zero
        store[half, 9] = zero
        main = field[:, half * 256 : half * 256 + 256].reshape(8, 64, 256)
        next_z = field[:, 256:384] if half == 0 else field[:, 128:256]
        turned = pltpu.roll(next_z, 64, 1).reshape(8, 64, 128)
        next_z = next_z.reshape(8, 64, 128)
        in_low, in_high = (next_z, turned) if half == 0 else (turned, next_z)
        for j in range(3):
            store[half, 1:9, :, j * 256 : (j + 1) * 256] = shift_y(main, j - 1).astype(BF16)
        edge = jnp.where(low, shift_y(in_low, -1), in_high)
        store[half, 1:9, :, 768:896] = edge.astype(BF16)
        store[half, 1:9, :, 896:960] = shift_y(in_low, 1)[:, :, :64].astype(BF16)


def widen_pairs(store, field):
    low = lane_of((512, 128)) < 64
    zero = jnp.zeros((64, 768), BF16)
    none = jnp.zeros((512, 128), F32)
    pairs = [field[:, p * 128 : (p + 1) * 128] for p in range(4)]
    turned = [none] + [pltpu.roll(p, 64, 1) for p in pairs] + [none]
    for p in range(4):
        store[p, 0] = zero
        store[p, 9] = zero
        near = jnp.where(low, turned[p], turned[p + 2])
        whole = jnp.concatenate([pairs[p], near], axis=1).reshape(8, 64, 256)
        for j in range(3):
            store[p, 1:9, :, j * 256 : (j + 1) * 256] = shift_y(whole, j - 1).astype(BF16)


def rows_of(store, half, i, first=0, count=8):
    return store[half, i + first : i + first + count].reshape(count * 64, 960)


def place_weights(w_hidden, ahead, back):
    lane = lane_of((64, 128))
    low = lane < 64
    zero = jnp.zeros((64, 128), BF16)
    tiles = [w_hidden[:, t * 128 : (t + 1) * 128] for t in range(13)]
    last = w_hidden[:, 1664:1728]
    tiles.append(jnp.concatenate([last, last], axis=1))
    tiles = [t.astype(F32) for t in tiles]
    swapped = [pltpu.roll(t, 64, 1) for t in tiles]
    lows, highs = [], []
    for j in range(9):
        t = 3 * j // 2
        if j % 2 == 0:
            ab = tiles[t]
            bc = jnp.where(low, swapped[t], swapped[t + 1])
            c_low, c_high = tiles[t + 1], swapped[t + 1]
            a_low, a_high = tiles[t], swapped[t]
        else:
            bc = tiles[t + 1]
            ab = jnp.where(low, swapped[t], swapped[t + 1])
            c_low, c_high = swapped[t + 1], tiles[t + 1]
            a_low, a_high = swapped[t], tiles[t]
        lows.append((c_low, a_low))
        highs.append((c_high, a_high))
        c_0 = jnp.where(low, c_low, 0.0).astype(BF16)
        o_a = jnp.where(low, 0.0, a_high).astype(BF16)
        ab = ab.astype(BF16)
        bc = bc.astype(BF16)
        rows = [(bc, zero), (ab, c_0), (o_a, bc), (zero, ab)]
        flip = 8 - j
        for half in range(2):
            for z in range(4):
                at = slice(z * 64, (z + 1) * 64)
                for part in range(2):
                    if ahead is not None:
                        start = (j % 3) * 256 + part * 128
                        ahead[half, j // 3, at, start : start + 128] = rows[z][part]
                        continue
                    start = (flip % 3) * 256 + z * 64
                    cut = slice(part * 128, (part + 1) * 128)
                    back[half, flip // 3, start : start + 64, cut] = rows[z][part]
        if ahead is not None:
            continue
        start = 768 + (flip % 3) * 64
        back[0, flip // 3, start : start + 64, 0:128] = zero
        back[0, flip // 3, start : start + 64, 128:256] = o_a
        back[1, flip // 3, start : start + 64, 0:128] = c_0
        back[1, flip // 3, start : start + 64, 128:256] = zero
    if ahead is None:
        return
    for half in range(2):
        for i in range(3):
            edge = jnp.where(low, lows[3 * i][half], highs[3 * i + 1][half]).astype(BF16)
            end = lows[3 * i + 2][half][:, :64].astype(BF16)
            for z in range(4):
                at = slice(z * 64, (z + 1) * 64)
                here = z == (3 if half == 0 else 0)
                ahead[half, i, at, 768:896] = edge if here else zero
                ahead[half, i, at, 896:960] = end if here else zero[:, :64]


def whole_kernel(*refs):
    sources, refs = refs[:9], refs[9:]
    (u_result, f_result, result), refs = refs[:3], refs[3:]
    held_in, refs = refs[:9], refs[9:]
    vel, target, w_first, w_hidden, w_last, owner, block, fixed, sel = held_in
    (
        u_next,
        filt, first_in, w_one, ahead, back, wide_act, wide_del, slope_one, pair_act, eddy_z,
        sums, first_sums, ext, y_out, y_in, z_out, z_in,
        half_in, half_sum, chunk_in, chunk_sum, deep_in, total,
        f_in, f_sum, f_plane, f_mid, f_deep, f_total,
        local_sems, sems,
    ) = refs

    loads = [
        pltpu.make_async_copy(src, dst, local_sems.at[n])
        for n, (src, dst) in enumerate(zip(sources, held_in))
    ]
    for n in (3, 0, 2, 8, 7, 1, 4, 5, 6):
        loads[n].start()

    moves = []

    def hand_over(src, dst):
        moves.append(pltpu.make_async_copy(src, dst, local_sems.at[9 + len(moves)]))
        moves[-1].start()

    gx, gy, role = lax.axis_index("gx"), lax.axis_index("gy"), lax.axis_index("role")
    depth, y = gx // 4, gx % 4
    x, core = (gy // 2) * 2 + role, gy % 2
    spot = y * 4 + x

    def plane(dy, dx):
        to_y, to_x = (y + dy) % 4, (x + dx) % 4
        return to_y * 4 + to_x, (depth * 4 + to_y, (to_x // 2) * 2 + core, to_x % 2)

    reach = (0, 1, 2, 1)
    steps = [(dy, dx) for dy in range(4) for dx in range(4) if dy or dx]
    steps.sort(key=lambda s: -reach[s[0]] - reach[s[1]])
    deeper = [(((depth + d) % 8) * 4 + y, gy, role) for d in (4, 3, 5, 2, 6, 1, 7)]
    other = (gx, gy - core + 1 - core, role)
    x_up, x_down = ((gx + 1) % 32, gy, role), ((gx + 31) % 32, gy, role)
    y_up, y_down = (gx, (gy + 1) % 4, role), (gx, (gy + 3) % 4, role)
    z_side = (gx, gy, 1 - role)

    barrier = pltpu.get_barrier_semaphore()
    greeted = [plane(dy, dx)[1] for dy, dx in steps] + deeper + [x_up, x_down, y_up, y_down]
    for device in greeted:
        pl.semaphore_signal(barrier, inc=1, device_id=device, device_id_type=MESH)

    started = []

    def send(src, dst, device):
        at = len(started)
        part = pltpu.make_async_remote_copy(
            src_ref=src, dst_ref=dst, send_sem=sems.at[0, at], recv_sem=sems.at[1, at],
            device_id=device, device_id_type=MESH,
        )
        started.append(part)
        part.start()
        return part

    for n in (3, 0, 2, 8, 7, 1, 4, 5, 6):
        loads[n].wait()
    place_weights(w_hidden, ahead, None)
    placed = dot(w_first[...], sel[...]).astype(BF16)
    for i in range(3):
        for zo in range(8):
            at = (i * 8 + zo) * 128
            w_one[i, zo * 64 : (zo + 1) * 64, :] = placed[:, at : at + 128]

    pooled = []
    for comp in range(3):
        summed = None
        for dx in range(2):
            for dy in range(2):
                part = jnp.concatenate(
                    [vel[comp, 2 * i + dx, pl.ds(dy, 8, stride=2), :] for i in range(8)], axis=0
                )
                summed = part if summed is None else summed + part
        pooled.append(summed)
    rest = jnp.concatenate(pooled, axis=1)
    blocks = None
    for _ in range(3):
        piece = rest.astype(BF16)
        rest = rest - piece.astype(F32)
        term = dot(piece, fixed[0:384])
        blocks = term if blocks is None else blocks + term
    blocks = blocks.astype(BF16).astype(F32)
    want = target[...].astype(F32).reshape(64, 64).astype(BF16)
    blocks = blocks + dot(want, fixed[384:448])
    for b in range(8):
        tile = blocks[:, (b // 4) * 128 : (b // 4) * 128 + 128]
        if b % 4:
            tile = pltpu.roll(tile, 128 - 32 * (b % 4), 1)
        filt[pl.ds(b, 64, stride=8), :] = tile
    held = filt[...]
    targets = dot(held.astype(BF16), fixed[448:576])
    lane = lane_of((512, 128))
    inputs = jnp.where(lane < 24, held, 0.0).reshape(8, 64, 128)
    near = shift_y(inputs, -1)
    near = near + pltpu.roll(inputs.reshape(512, 128), 32, 1).reshape(8, 64, 128)
    near = near + pltpu.roll(shift_y(inputs, 1).reshape(512, 128), 64, 1).reshape(8, 64, 128)
    first_in[0] = jnp.zeros((64, 128), BF16)
    first_in[9] = jnp.zeros((64, 128), BF16)
    first_in[1:9] = near.astype(BF16)

    pre = None
    for i in range(3):
        term = dot(first_in[i : i + 8].reshape(512, 128), w_one[i], NT)
        pre = term if pre is None else pre + term
    sig = 1.0 / (1.0 + jnp.exp(-pre))
    slope_one[...] = sig * (1.0 + pre * (1.0 - sig))
    acts = (pre * sig).astype(BF16).astype(F32)
    widen(wide_act, acts)

    wl = w_last[...].astype(F32)
    wl = jnp.concatenate([wl, wl, wl, wl], axis=1)
    rows_iota = lax.broadcasted_iota(jnp.int32, (128, 256), 0)
    lanes_iota = lax.broadcasted_iota(jnp.int32, (128, 256), 1)
    out_map = jnp.where(rows_iota // 2 % 4 == lanes_iota // 64, wl, 0.0).astype(BF16)
    repeat = jnp.where(rows_iota == lanes_iota // 64 * 2, 1.0, 0.0).astype(BF16)

    number = lax.broadcasted_iota(jnp.int32, (8, 256), 0)
    drawn = jnp.where((owner[...] == gx) & (block[...] == number), 1.0, 0.0)
    times = jnp.sum(drawn, axis=1, keepdims=True)

    loss = jnp.zeros((8, 128), F32)
    last = jnp.zeros((8, 256), F32)

    def second_layer(half, quarter):
        pre = None
        for i in range(3):
            term = dot(rows_of(wide_act, half, i, 4 * quarter, 4), ahead[half, i], NT)
            pre = term if pre is None else pre + term
        return pre

    turns = [(half, quarter) for half in range(2) for quarter in range(2)]
    found = []
    deltas, parts = [[], []], [[], [], [], []]
    for turn, (half, quarter) in enumerate(turns):
        while len(found) < min(4, turn + 1 + 2):
            found.append(second_layer(*turns[len(found)]))
            if len(found) == 2:
                widen_pairs(pair_act, acts)
        pre = found[turn]
        here = slice(quarter * 256, quarter * 256 + 256)
        sig = 1.0 / (1.0 + jnp.exp(-pre))
        act = (pre * sig).astype(BF16)
        slope = sig * (1.0 + pre * (1.0 - sig))
        logits = dot(act, out_map, NT)
        small = jnp.exp(-jnp.abs(logits))
        eddy = 0.5 * (jnp.maximum(logits, 0.0) + jnp.log1p(small))
        eddy_z[half, here] = eddy
        gate = jnp.where(logits >= 0, 1.0, small) / (1.0 + small)
        error = eddy - targets[here, half * 128 : half * 128 + 128]
        loss = loss + jnp.sum((error * error).reshape(32, 8, 128), axis=0)
        d_logit = dot((error * gate * (1.0 / (256 * 512))).astype(BF16), repeat)
        last = last + jnp.sum((d_logit * act.astype(F32)).reshape(32, 8, 256), axis=0)
        delta = (wl * d_logit * slope).astype(BF16).astype(F32)
        deltas[half].append(delta)
        scaled = (delta.reshape(32, 8, 256) * times.reshape(1, 8, 1)).reshape(256, 256)
        high = scaled.astype(BF16)
        low = (scaled - high.astype(F32)).astype(BF16)
        for p in range(2):
            cut = slice(p * 128, p * 128 + 128)
            parts[2 * half + p].append(jnp.concatenate([high[:, cut].T, low[:, cut].T], axis=0))

    per_block = jnp.sum(loss, axis=1, keepdims=True) * (1.0 / (32 * 512))
    by_slot = jnp.sum(drawn * per_block, axis=0, keepdims=True)
    group = gy * 2 + role
    at = lax.broadcasted_iota(jnp.int32, (64, 128), 0)
    by_slot = jnp.where(at % 2 == 0, by_slot[:, :128], by_slot[:, 128:])
    sums[0, 448:512, :] = jnp.where(at // 2 == group, by_slot, 0.0)
    last = jnp.sum(last * times, axis=0, keepdims=True)
    last = last[:, :128] + last[:, 128:]
    last = last + pltpu.roll(last, 64, 1)
    sums[1, 448:512, :] = jnp.broadcast_to(last, (64, 128))

    def column(t, value):
        sums[t // 7, (t % 7) * 64 : (t % 7) * 64 + 64, :] = value

    lane = lane_of((64, 128))
    is_low = lane < 64
    held_a = None

    def shift_sums(i):
        grad = None
        for p in range(4):
            term = dot(
                jnp.concatenate(parts[p], axis=1), pair_act[p, i : i + 8].reshape(512, 768)
            )
            grad = term if grad is None else grad + term
        return grad[:128] + grad[128:]

    grads = [shift_sums(0)]
    for i in range(3):
        if i < 2:
            grads.append(shift_sums(i + 1))
        grad = grads[i]
        for j in range(3):
            k = 3 * i + j
            g = [
                [grad[zo * 64 : zo * 64 + 64, j * 256 + p * 128 : j * 256 + p * 128 + 128] for p in range(2)]
                for zo in range(2)
            ]
            cb = pltpu.roll(g[0][0], 64, 1)
            ab = g[1][0] + jnp.where(is_low, g[0][1], cb)
            c_low = cb + pltpu.roll(g[1][1], 64, 1)
            t = 3 * k // 2
            if k % 2 == 0:
                column(t, ab)
                held_a = c_low
            else:
                ba = pltpu.roll(ab, 64, 1)
                column(t, jnp.where(is_low, held_a, ba))
                column(t + 1, jnp.where(is_low, ba, pltpu.roll(c_low, 64, 1)))
    column(13, jnp.where(is_low, held_a, 0.0))
    pl.semaphore_wait(barrier, len(greeted))
    first = send(sums.at[1 - core], half_in, other)

    slot_of, base_of = (0, 0, 1, 2), (0, 16, 0, 0)
    lane16 = lane_of((16, 128))

    def pack_sides(c, field, wide):
        for h in range(wide):
            for i in range(16):
                low, high = field[i, h : h + 1, :], field[i, 16 - wide + h : 17 - wide + h, :]
                y_out[0, 2 * c + h, i : i + 1, :] = low
                y_out[1, 2 * c + h, i : i + 1, :] = high
        packed = None
        for i in range(16):
            g = base_of[c] + i
            moved = pltpu.roll(field[i], 2 + 4 * g, 1)
            packed = moved if packed is None else jnp.where(lane16 // 4 == g, moved, packed)
        return packed

    sides_of = [pack_sides(c, vel.at[c], 2) for c in range(3)]
    z_out[0] = jnp.where(lane16 < 64, sides_of[0], sides_of[1])
    z_out[1] = sides_of[2]

    field = jnp.zeros((64, 128), F32)
    for half in range(2):
        for b in range(8):
            part = eddy_z[half, pl.ds(b, 64, stride=8), :]
            field = jnp.where(lane // 8 == 2 * b + half, part, field)
    field = 0.02 + field
    for i in range(8):
        for dx in range(2):
            for dy in range(2):
                ext[3, 2 + 2 * i + dx, pl.ds(8 + dy, 8, stride=2), :] = field[i * 8 : i * 8 + 8]
    z_out[2] = pack_sides(3, ext.at[3, 2:18, 8:24], 1)
    rims = [
        send(vel.at[:, 0:2], ext.at[0:3, 18:20, 8:24], x_down),
        send(vel.at[:, 14:16], ext.at[0:3, 0:2, 8:24], x_up),
        send(ext.at[3, 2:3, 8:24], ext.at[3, 18:19, 8:24], x_down),
        send(ext.at[3, 17:18, 8:24], ext.at[3, 1:2, 8:24], x_up),
        send(y_out.at[0], y_in.at[1], y_down),
        send(y_out.at[1], y_in.at[0], y_up),
        send(z_out, z_in, z_side),
    ]

    place_weights(w_hidden, None, back)
    widen(wide_del, jnp.concatenate([jnp.concatenate(d, axis=0) for d in deltas], axis=1))
    scatter = []
    first.wait_recv()
    half_sum[...] = sums[core] + half_in[...]
    for s, (dy, dx) in enumerate(steps):
        to, device = plane(dy, dx)
        scatter.append(
            send(half_sum.at[pl.ds(pl.multiple_of(to * 32, 32), 32)], chunk_in.at[s], device)
        )

    firsts = []
    for half in range(2):
        d_act = None
        for i in range(3):
            term = dot(rows_of(wide_del, half, i), back[half, i])
            d_act = term if d_act is None else d_act + term
        d_first = (d_act * slope_one[:, half * 256 : half * 256 + 256]).astype(BF16).astype(F32)
        scaled = (d_first.reshape(64, 8, 256) * times.reshape(1, 8, 1)).reshape(512, 256)
        high = scaled.astype(BF16)
        low = (scaled - high.astype(F32)).astype(BF16)
        firsts.append((high.T, low.T))
    lhs = jnp.concatenate([firsts[0][0], firsts[1][0], firsts[0][1], firsts[1][1]], axis=0)
    packed = jnp.zeros((64, 128), F32)
    for i in range(3):
        grad = dot(lhs, first_in[i : i + 8].reshape(512, 128))
        grad = grad[:512] + grad[512:]
        summed = None
        for zo in range(8):
            part = grad[zo * 64 : zo * 64 + 64]
            shift = (-3 * (zo - 1)) % 128
            part = pltpu.roll(part, shift, 1) if shift else part
            summed = part if summed is None else summed + part
        for j in range(3):
            start = 9 * (3 * i + j)
            shift = (start - 32 * j) % 128
            moved = pltpu.roll(summed, shift, 1) if shift else summed
            packed = jnp.where((lane >= start) & (lane < start + 9), moved, packed)
    first_sums[...] = packed

    own32 = pl.ds(pl.multiple_of(core * 32, 32), 32)
    f_first = send(
        first_sums.at[pl.ds(pl.multiple_of((1 - core) * 32, 32), 32)], f_in, other
    )
    ext[0:3, 2:18, 8:24, :] = vel[...]
    f_first.wait_recv()
    mine = first_sums[own32, :] + f_in[...]
    f_sum[...] = mine
    f_plane[spot] = mine
    f_across = [send(f_sum, f_plane.at[spot], plane(dy, dx)[1]) for dy, dx in steps]

    for part in scatter:
        part.wait_recv()
    mine = half_sum[pl.ds(pl.multiple_of(spot * 32, 32), 32), :]
    for s in range(15):
        mine = mine + chunk_in[s]
    chunk_sum[...] = mine
    deep_in[depth] = mine
    deep = [send(chunk_sum, deep_in.at[depth], device) for device in deeper]

    for rim in rims:
        rim.wait_recv()
    for c in range(4):
        for h in range(1 if c == 3 else 2):
            for i in range(16):
                to = 7 if c == 3 else 6 + h
                ext[c, 2 + i, to : to + 1, :] = y_in[0, 2 * c + h, i : i + 1, :]
                ext[c, 2 + i, 24 + h : 25 + h, :] = y_in[1, 2 * c + h, i : i + 1, :]

    def row(i, carry):
        def beside(c, here, far):
            turn = (254 - 4 * (base_of[c] + i)) % 128
            edge = pltpu.roll(z_in[slot_of[c]], turn, 1)
            out = []
            for m in (1, 2) if far else (1,):
                after = jnp.where(lane16 < m, edge, here)
                before = jnp.where(lane16 >= 128 - m, edge, here)
                out += [pltpu.roll(after, 128 - m, 1), pltpu.roll(before, m, 1)]
            return out

        centre = ext[3, 2 + i, 8:24, :]
        sides = [
            (ext[3, 3 + i, 8:24, :], ext[3, 1 + i, 8:24, :]),
            (ext[3, 2 + i, 9:25, :], ext[3, 2 + i, 7:23, :]),
            beside(3, centre, False),
        ]
        sides = [(0.5 * (centre + a), 0.5 * (centre + b)) for a, b in sides]
        speed = [ext[c, 2 + i, 8:24, :] for c in range(3)]
        for c in range(3):
            here = speed[c]
            near = [
                [ext[c, 2 + i + m, 8:24, :] for m in (1, -1, 2, -2)],
                [ext[c, 2 + i, 8 + m : 24 + m, :] for m in (1, -1, 2, -2)],
                beside(c, here, True),
            ]
            change = None
            for axis in range(3):
                a1, b1, a2, b2 = near[axis]
                slope = (8.0 * (a1 - b1) - (a2 - b2)) * (1.0 / 12.0)
                term = sides[axis][0] * (a1 - here) - sides[axis][1] * (here - b1)
                term = term - speed[axis] * slope
                change = term if change is None else change + term
            u_next[c, i] = here + 0.2 * change
        return carry

    lax.fori_loop(0, 16, row, 0)
    hand_over(u_next, u_result)

    for part in f_across:
        part.wait_recv()
    mine = f_plane[0]
    for s in range(1, 16):
        mine = mine + f_plane[s]
    f_mid[...] = mine
    f_deep[depth] = mine
    f_planes = [send(f_mid, f_deep.at[depth], device) for device in deeper]

    for part in deep:
        part.wait_recv()
    mine = deep_in[0]
    for d in range(1, 8):
        mine = mine + deep_in[d]
    own = pl.ds(pl.multiple_of(spot * 32, 32), 32)
    total[core, own, :] = mine
    gather = [
        send(total.at[core, own], total.at[core, own], plane(dy, dx)[1]) for dy, dx in steps
    ]

    for part in f_planes:
        part.wait_recv()
    mine = f_deep[0]
    for d in range(1, 8):
        mine = mine + f_deep[d]
    f_total[own32, :] = mine
    f_last = send(f_total.at[own32], f_result.at[own32], other)
    hand_over(f_total.at[own32], f_result.at[own32])

    across = []
    for dy in range(4):
        for part, (sy, _) in zip(gather, steps):
            if sy == dy:
                part.wait_recv()
        rows = pl.ds(pl.multiple_of(((y + 4 - dy) % 4) * 128, 128), 128)
        across.append(send(total.at[core, rows], result.at[core, rows], other))
    hand_over(total.at[core], result.at[core])
    f_last.wait_recv()
    for part in across:
        part.wait_recv()
    for part in started:
        part.wait_send()
    for move in moves:
        move.wait()


SENDS = 7 + 1 + 15 + 1 + 15 + 7 + 7 + 15 + 1 + 4


def out_shapes():
    return (
        jax.ShapeDtypeStruct((3, 16, 16, 128), F32),
        jax.ShapeDtypeStruct((1, 1, 8), F32),
        jax.ShapeDtypeStruct((64, 81), F32),
        jax.ShapeDtypeStruct((64, 1728), F32),
        jax.ShapeDtypeStruct((1, 64), F32),
    )


def hand_out(
    u_source, f_source, source, u_result, loss_result, first_result, hidden_result, last_result,
    u_held, f_held, held, slot_loss, grad_first, grad_hidden, grad_last, sems,
):
    gx, gy, role = lax.axis_index("gx"), lax.axis_index("gy"), lax.axis_index("role")
    loads = [pltpu.make_async_copy(source.at[n], held.at[n], sems.at[n]) for n in range(2)]
    loads += [pltpu.make_async_copy(u_source.at[n], u_held.at[n], sems.at[2 + n]) for n in range(3)]
    loads.append(pltpu.make_async_copy(f_source, f_held, sems.at[5]))
    stores = [pltpu.make_async_copy(u_held.at[n], u_result.at[n], sems.at[6 + n]) for n in range(3)]
    stores += [
        pltpu.make_async_copy(grad_hidden, hidden_result, sems.at[9]),
        pltpu.make_async_copy(grad_first, first_result, sems.at[10]),
        pltpu.make_async_copy(grad_last, last_result, sems.at[11]),
        pltpu.make_async_copy(slot_loss, loss_result, sems.at[12]),
    ]
    for load in loads:
        load.start()
    for half in range(2):
        loads[half].wait()
        for t in range(7):
            start, width = half * 896 + t * 128, 64 if half == 1 and t == 6 else 128
            grad_hidden[:, start : start + width] = held[half, t * 64 : t * 64 + 64, :width]
    stores[3].start()
    for n in range(3):
        loads[2 + n].wait()
        stores[n].start()
    loads[5].wait()
    grad_first[...] = f_held[:, :81]
    grad_last[...] = held[1, 448:449, :64]
    losses = held[0, 448:464, :]
    at = lax.broadcasted_iota(jnp.int32, (16, 128), 0)
    losses = jnp.where(at == (gy * 2 + role) * 2 + gx // 16, losses, 0.0)
    losses = jnp.sum(losses, axis=0, keepdims=True)
    losses = pltpu.roll(losses, (128 - (gx % 16) * 8) % 128, 1)
    slot_loss[0] = losses[:, :8]
    for store in stores[4:]:
        store.start()
    for store in stores:
        store.wait()


def on_device(velocity, target_visc, w_first, w_hidden, w_last, sample_owner, sample_block):
    anywhere = pl.BlockSpec(memory_space=pl.ANY)
    spread = spread_matrix()
    rows = (pool_matrix(), target_matrix(), spread, spread[:8])
    consts = [jnp.asarray(np.concatenate(rows, 0)), jnp.asarray(first_selector())]
    args = [
        velocity, target_visc, w_first, w_hidden, w_last.reshape(1, 64),
        sample_owner.reshape(1, 256), sample_block.reshape(1, 256), *consts,
    ]
    sums = [
        jax.ShapeDtypeStruct(shape, F32) for shape in ((3, 16, 16, 128), (64, 128), (2, 512, 128))
    ]
    outs = pl.pallas_call(
        whole_kernel,
        out_shape=sums,
        in_specs=[anywhere] * 9,
        out_specs=(anywhere,) * 3,
        scratch_shapes=[pltpu.VMEM(a.shape, a.dtype) for a in args] + [
            pltpu.VMEM((3, 16, 16, 128), F32),
            pltpu.VMEM((512, 128), F32),
            pltpu.VMEM((10, 64, 128), BF16),
            pltpu.VMEM((3, 512, 128), BF16),
            pltpu.VMEM((2, 3, 256, 960), BF16),
            pltpu.VMEM((2, 3, 960, 256), BF16),
            pltpu.VMEM((2, 10, 64, 960), BF16),
            pltpu.VMEM((2, 10, 64, 960), BF16),
            pltpu.VMEM((512, 512), F32),
            pltpu.VMEM((4, 10, 64, 768), BF16),
            pltpu.VMEM((2, 512, 128), F32),
            pltpu.VMEM((2, 512, 128), F32),
            pltpu.VMEM((64, 128), F32),
            pltpu.VMEM((4, 20, 32, 128), F32),
            pltpu.VMEM((2, 7, 16, 128), F32),
            pltpu.VMEM((2, 7, 16, 128), F32),
            pltpu.VMEM((3, 16, 128), F32),
            pltpu.VMEM((3, 16, 128), F32),
            pltpu.VMEM((512, 128), F32),
            pltpu.VMEM((512, 128), F32),
            pltpu.VMEM((15, 32, 128), F32),
            pltpu.VMEM((32, 128), F32),
            pltpu.VMEM((8, 32, 128), F32),
            pltpu.VMEM((2, 512, 128), F32),
            pltpu.VMEM((32, 128), F32),
            pltpu.VMEM((32, 128), F32),
            pltpu.VMEM((16, 32, 128), F32),
            pltpu.VMEM((32, 128), F32),
            pltpu.VMEM((8, 32, 128), F32),
            pltpu.VMEM((64, 128), F32),
            pltpu.SemaphoreType.DMA((12,)),
            pltpu.SemaphoreType.DMA((2, SENDS)),
        ],
        compiler_params=pltpu.CompilerParams(
            vmem_limit_bytes=60 * 1024 * 1024, collective_id=0, has_side_effects=True
        ),
        name="whole",
    )(*args)
    outs = pl.pallas_call(
        hand_out,
        out_shape=out_shapes(),
        in_specs=[anywhere] * 3,
        out_specs=(anywhere,) * 5,
        scratch_shapes=[pltpu.VMEM(a.shape, a.dtype) for a in [*sums, *out_shapes()[1:]]]
        + [pltpu.SemaphoreType.DMA((13,))],
        compiler_params=pltpu.CompilerParams(vmem_limit_bytes=60 * 1024 * 1024),
        name="hand_out",
    )(*outs)
    u_next, slot_loss, grad_first, grad_hidden, grad_last = outs
    return (u_next, slot_loss, grad_first, grad_hidden, grad_last.reshape(64))


def solution(mesh):
    return jax.shard_map(
        on_device,
        mesh=mesh,
        in_specs=(
            P(None, "gx", "gy", "role"),
            P("gx", "gy", "role"),
            P(),
            P(),
            P(),
            P("gy", "role", None, None),
            P("gy", "role", None, None),
        ),
        out_specs=(P(None, "gx", "gy", "role"), P("gy", "role", "gx"), P(), P(), P()),
        check_vma=False,
    )
```

```python
import numpy as np
import jax
import jax.numpy as jnp
from jax import lax
from jax.sharding import PartitionSpec as P
from jax.experimental import pallas as pl
from jax.experimental.pallas import tpu as pltpu

SIDE = 8
CH = 64
F32 = jnp.float32
BF16 = jnp.bfloat16
NT = (((1,), (1,)), ((), ()))
NN = (((1,), (0,)), ((), ()))
MESH = pl.DeviceIdType.MESH


def dot(a, b, dims=NN):
    return lax.dot_general(a, b, dims, preferred_element_type=F32)


def pool_matrix():
    z = np.arange(128)[:, None]
    lane = np.arange(256)[None, :]
    block, inner = lane // 32, lane % 32
    parts = []
    for comp in range(3):
        hit = (inner < 24) & (inner % 3 == comp) & (z // 2 == block * 8 + inner // 3)
        parts.append(np.where(hit, 0.125, 0.0))
    return np.concatenate(parts, 0).astype(jnp.bfloat16)


def target_matrix():
    z = np.arange(64)[:, None]
    lane = np.arange(256)[None, :]
    block, inner = lane // 32, lane % 32
    return ((inner >= 24) & (z == block * 8 + inner - 24)).astype(jnp.bfloat16)


def spread_matrix():
    row = np.arange(128)[:, None]
    lane = np.arange(256)[None, :]
    return (row == 24 + lane // 128 * 4 + lane // 2 % 4).astype(jnp.bfloat16)


def first_selector():
    out = np.zeros((81, 3, 8, 128), np.float32)
    for i in range(3):
        for zo in range(8):
            for j in range(3):
                for t in range(9):
                    zi = zo - 1 + t // 3
                    if 0 <= zi < 8:
                        out[9 * (3 * i + j) + t, i, zo, j * 32 + zi * 3 + t % 3] = 1.0
    return out.reshape(81, 3072).astype(jnp.bfloat16)


def lane_of(shape):
    return lax.broadcasted_iota(jnp.int32, shape, len(shape) - 1)


def shift_y(field, shift):
    zero = jnp.zeros((8, 8, field.shape[2]), field.dtype)
    if shift < 0:
        return jnp.concatenate([zero, field[:, :56]], axis=1)
    if shift > 0:
        return jnp.concatenate([field[:, 8:], zero], axis=1)
    return field


def widen(store, field):
    low = lane_of((8, 64, 128)) < 64
    zero = jnp.zeros((64, 960), BF16)
    for half in range(2):
        store[half, 0] = zero
        store[half, 9] = zero
        main = field[:, half * 256 : half * 256 + 256].reshape(8, 64, 256)
        next_z = field[:, 256:384] if half == 0 else field[:, 128:256]
        turned = pltpu.roll(next_z, 64, 1).reshape(8, 64, 128)
        next_z = next_z.reshape(8, 64, 128)
        in_low, in_high = (next_z, turned) if half == 0 else (turned, next_z)
        for j in range(3):
            store[half, 1:9, :, j * 256 : (j + 1) * 256] = shift_y(main, j - 1).astype(BF16)
        edge = jnp.where(low, shift_y(in_low, -1), in_high)
        store[half, 1:9, :, 768:896] = edge.astype(BF16)
        store[half, 1:9, :, 896:960] = shift_y(in_low, 1)[:, :, :64].astype(BF16)


def widen_pairs(store, field):
    low = lane_of((512, 128)) < 64
    zero = jnp.zeros((64, 768), BF16)
    none = jnp.zeros((512, 128), F32)
    pairs = [field[:, p * 128 : (p + 1) * 128] for p in range(4)]
    turned = [none] + [pltpu.roll(p, 64, 1) for p in pairs] + [none]
    for p in range(4):
        store[p, 0] = zero
        store[p, 9] = zero
        near = jnp.where(low, turned[p], turned[p + 2])
        whole = jnp.concatenate([pairs[p], near], axis=1).reshape(8, 64, 256)
        for j in range(3):
            store[p, 1:9, :, j * 256 : (j + 1) * 256] = shift_y(whole, j - 1).astype(BF16)


def rows_of(store, half, i, first=0, count=8):
    return store[half, i + first : i + first + count].reshape(count * 64, 960)


def place_weights(w_hidden, ahead, back):
    lane = lane_of((64, 128))
    low = lane < 64
    zero = jnp.zeros((64, 128), BF16)
    tiles = [w_hidden[:, t * 128 : (t + 1) * 128] for t in range(13)]
    last = w_hidden[:, 1664:1728]
    tiles.append(jnp.concatenate([last, last], axis=1))
    tiles = [t.astype(F32) for t in tiles]
    swapped = [pltpu.roll(t, 64, 1) for t in tiles]
    lows, highs = [], []
    for j in range(9):
        t = 3 * j // 2
        if j % 2 == 0:
            ab = tiles[t]
            bc = jnp.where(low, swapped[t], swapped[t + 1])
            c_low, c_high = tiles[t + 1], swapped[t + 1]
            a_low, a_high = tiles[t], swapped[t]
        else:
            bc = tiles[t + 1]
            ab = jnp.where(low, swapped[t], swapped[t + 1])
            c_low, c_high = swapped[t + 1], tiles[t + 1]
            a_low, a_high = swapped[t], tiles[t]
        lows.append((c_low, a_low))
        highs.append((c_high, a_high))
        c_0 = jnp.where(low, c_low, 0.0).astype(BF16)
        o_a = jnp.where(low, 0.0, a_high).astype(BF16)
        ab = ab.astype(BF16)
        bc = bc.astype(BF16)
        rows = [(bc, zero), (ab, c_0), (o_a, bc), (zero, ab)]
        flip = 8 - j
        for half in range(2):
            for z in range(4):
                at = slice(z * 64, (z + 1) * 64)
                for part in range(2):
                    if ahead is not None:
                        start = (j % 3) * 256 + part * 128
                        ahead[half, j // 3, at, start : start + 128] = rows[z][part]
                        continue
                    start = (flip % 3) * 256 + z * 64
                    cut = slice(part * 128, (part + 1) * 128)
                    back[half, flip // 3, start : start + 64, cut] = rows[z][part]
        if ahead is not None:
            continue
        start = 768 + (flip % 3) * 64
        back[0, flip // 3, start : start + 64, 0:128] = zero
        back[0, flip // 3, start : start + 64, 128:256] = o_a
        back[1, flip // 3, start : start + 64, 0:128] = c_0
        back[1, flip // 3, start : start + 64, 128:256] = zero
    if ahead is None:
        return
    for half in range(2):
        for i in range(3):
            edge = jnp.where(low, lows[3 * i][half], highs[3 * i + 1][half]).astype(BF16)
            end = lows[3 * i + 2][half][:, :64].astype(BF16)
            for z in range(4):
                at = slice(z * 64, (z + 1) * 64)
                here = z == (3 if half == 0 else 0)
                ahead[half, i, at, 768:896] = edge if here else zero
                ahead[half, i, at, 896:960] = end if here else zero[:, :64]


def whole_kernel(*refs):
    sources, refs = refs[:9], refs[9:]
    (u_result, f_result, result), refs = refs[:3], refs[3:]
    held_in, refs = refs[:9], refs[9:]
    vel, target, w_first, w_hidden, w_last, owner, block, fixed, sel = held_in
    (
        u_next,
        filt, first_in, w_one, ahead, back, wide_act, wide_del, slope_one, pair_act, eddy_z,
        sums, first_sums, ext, y_out, y_in, z_out, z_in,
        half_in, half_sum, chunk_in, chunk_sum, deep_in, total,
        f_in, f_sum, f_plane, f_mid, f_deep, f_total,
        local_sems, sems,
    ) = refs

    loads = [
        pltpu.make_async_copy(src, dst, local_sems.at[n])
        for n, (src, dst) in enumerate(zip(sources, held_in))
    ]
    for n in (3, 0, 2, 8, 7, 1, 4, 5, 6):
        loads[n].start()

    moves = []

    def hand_over(src, dst):
        moves.append(pltpu.make_async_copy(src, dst, local_sems.at[9 + len(moves)]))
        moves[-1].start()

    gx, gy, role = lax.axis_index("gx"), lax.axis_index("gy"), lax.axis_index("role")
    depth, y = gx // 4, gx % 4
    x, core = (gy // 2) * 2 + role, gy % 2
    spot = y * 4 + x

    def plane(dy, dx):
        to_y, to_x = (y + dy) % 4, (x + dx) % 4
        return to_y * 4 + to_x, (depth * 4 + to_y, (to_x // 2) * 2 + core, to_x % 2)

    reach = (0, 1, 2, 1)
    steps = [(dy, dx) for dy in range(4) for dx in range(4) if dy or dx]
    steps.sort(key=lambda s: -reach[s[0]] - reach[s[1]])
    deeper = [(((depth + d) % 8) * 4 + y, gy, role) for d in (4, 3, 5, 2, 6, 1, 7)]
    other = (gx, gy - core + 1 - core, role)
    x_up, x_down = ((gx + 1) % 32, gy, role), ((gx + 31) % 32, gy, role)
    y_up, y_down = (gx, (gy + 1) % 4, role), (gx, (gy + 3) % 4, role)
    z_side = (gx, gy, 1 - role)

    barrier = pltpu.get_barrier_semaphore()
    greeted = [plane(dy, dx)[1] for dy, dx in steps] + deeper + [x_up, x_down, y_up, y_down]
    for device in greeted:
        pl.semaphore_signal(barrier, inc=1, device_id=device, device_id_type=MESH)

    started = []

    def send(src, dst, device):
        at = len(started)
        part = pltpu.make_async_remote_copy(
            src_ref=src, dst_ref=dst, send_sem=sems.at[0, at], recv_sem=sems.at[1, at],
            device_id=device, device_id_type=MESH,
        )
        started.append(part)
        part.start()
        return part

    loads[3].wait()
    place_weights(w_hidden, ahead, None)
    for n in (0, 2, 8, 7, 1, 4, 5, 6):
        loads[n].wait()
    placed = dot(w_first[...], sel[...]).astype(BF16)
    for i in range(3):
        for zo in range(8):
            at = (i * 8 + zo) * 128
            w_one[i, zo * 64 : (zo + 1) * 64, :] = placed[:, at : at + 128]

    pooled = []
    for comp in range(3):
        summed = None
        for dx in range(2):
            for dy in range(2):
                part = jnp.concatenate(
                    [vel[comp, 2 * i + dx, pl.ds(dy, 8, stride=2), :] for i in range(8)], axis=0
                )
                summed = part if summed is None else summed + part
        pooled.append(summed)
    rest = jnp.concatenate(pooled, axis=1)
    blocks = None
    for _ in range(3):
        piece = rest.astype(BF16)
        rest = rest - piece.astype(F32)
        term = dot(piece, fixed[0:384])
        blocks = term if blocks is None else blocks + term
    blocks = blocks.astype(BF16).astype(F32)
    want = target[...].astype(F32).reshape(64, 64).astype(BF16)
    blocks = blocks + dot(want, fixed[384:448])
    for b in range(8):
        tile = blocks[:, (b // 4) * 128 : (b // 4) * 128 + 128]
        if b % 4:
            tile = pltpu.roll(tile, 128 - 32 * (b % 4), 1)
        filt[pl.ds(b, 64, stride=8), :] = tile
    held = filt[...]
    targets = dot(held.astype(BF16), fixed[448:576])
    lane = lane_of((512, 128))
    inputs = jnp.where(lane < 24, held, 0.0).reshape(8, 64, 128)
    near = shift_y(inputs, -1)
    near = near + pltpu.roll(inputs.reshape(512, 128), 32, 1).reshape(8, 64, 128)
    near = near + pltpu.roll(shift_y(inputs, 1).reshape(512, 128), 64, 1).reshape(8, 64, 128)
    first_in[0] = jnp.zeros((64, 128), BF16)
    first_in[9] = jnp.zeros((64, 128), BF16)
    first_in[1:9] = near.astype(BF16)

    pre = None
    for i in range(3):
        term = dot(first_in[i : i + 8].reshape(512, 128), w_one[i], NT)
        pre = term if pre is None else pre + term
    sig = 1.0 / (1.0 + jnp.exp(-pre))
    slope_one[...] = sig * (1.0 + pre * (1.0 - sig))
    acts = (pre * sig).astype(BF16).astype(F32)
    widen(wide_act, acts)

    wl = w_last[...].astype(F32)
    wl = jnp.concatenate([wl, wl, wl, wl], axis=1)
    rows_iota = lax.broadcasted_iota(jnp.int32, (128, 256), 0)
    lanes_iota = lax.broadcasted_iota(jnp.int32, (128, 256), 1)
    out_map = jnp.where(rows_iota // 2 % 4 == lanes_iota // 64, wl, 0.0).astype(BF16)
    repeat = jnp.where(rows_iota == lanes_iota // 64 * 2, 1.0, 0.0).astype(BF16)

    number = lax.broadcasted_iota(jnp.int32, (8, 256), 0)
    drawn = jnp.where((owner[...] == gx) & (block[...] == number), 1.0, 0.0)
    times = jnp.sum(drawn, axis=1, keepdims=True)

    loss = jnp.zeros((8, 128), F32)
    last = jnp.zeros((8, 256), F32)

    def second_layer(half, quarter):
        pre = None
        for i in range(3):
            term = dot(rows_of(wide_act, half, i, 4 * quarter, 4), ahead[half, i], NT)
            pre = term if pre is None else pre + term
        return pre

    turns = [(half, quarter) for half in range(2) for quarter in range(2)]
    found = []
    deltas, parts = [[], []], [[], [], [], []]
    for turn, (half, quarter) in enumerate(turns):
        while len(found) < min(4, turn + 1 + 2):
            found.append(second_layer(*turns[len(found)]))
            if len(found) == 2:
                widen_pairs(pair_act, acts)
        pre = found[turn]
        here = slice(quarter * 256, quarter * 256 + 256)
        sig = 1.0 / (1.0 + jnp.exp(-pre))
        act = (pre * sig).astype(BF16)
        slope = sig * (1.0 + pre * (1.0 - sig))
        logits = dot(act, out_map, NT)
        small = jnp.exp(-jnp.abs(logits))
        eddy = 0.5 * (jnp.maximum(logits, 0.0) + jnp.log1p(small))
        eddy_z[half, here] = eddy
        gate = jnp.where(logits >= 0, 1.0, small) / (1.0 + small)
        error = eddy - targets[here, half * 128 : half * 128 + 128]
        loss = loss + jnp.sum((error * error).reshape(32, 8, 128), axis=0)
        d_logit = dot((error * gate * (1.0 / (256 * 512))).astype(BF16), repeat)
        last = last + jnp.sum((d_logit * act.astype(F32)).reshape(32, 8, 256), axis=0)
        delta = (wl * d_logit * slope).astype(BF16).astype(F32)
        deltas[half].append(delta)
        scaled = (delta.reshape(32, 8, 256) * times.reshape(1, 8, 1)).reshape(256, 256)
        high = scaled.astype(BF16)
        low = (scaled - high.astype(F32)).astype(BF16)
        for p in range(2):
            cut = slice(p * 128, p * 128 + 128)
            parts[2 * half + p].append(jnp.concatenate([high[:, cut].T, low[:, cut].T], axis=0))

    per_block = jnp.sum(loss, axis=1, keepdims=True) * (1.0 / (32 * 512))
    by_slot = jnp.sum(drawn * per_block, axis=0, keepdims=True)
    group = gy * 2 + role
    at = lax.broadcasted_iota(jnp.int32, (64, 128), 0)
    by_slot = jnp.where(at % 2 == 0, by_slot[:, :128], by_slot[:, 128:])
    sums[0, 448:512, :] = jnp.where(at // 2 == group, by_slot, 0.0)
    last = jnp.sum(last * times, axis=0, keepdims=True)
    last = last[:, :128] + last[:, 128:]
    last = last + pltpu.roll(last, 64, 1)
    sums[1, 448:512, :] = jnp.broadcast_to(last, (64, 128))

    def column(t, value):
        sums[t // 7, (t % 7) * 64 : (t % 7) * 64 + 64, :] = value

    lane = lane_of((64, 128))
    is_low = lane < 64
    held_a = None

    def shift_sums(i):
        grad = None
        for p in range(4):
            term = dot(
                jnp.concatenate(parts[p], axis=1), pair_act[p, i : i + 8].reshape(512, 768)
            )
            grad = term if grad is None else grad + term
        return grad[:128] + grad[128:]

    grads = [shift_sums(0)]
    for i in range(3):
        if i < 2:
            grads.append(shift_sums(i + 1))
        grad = grads[i]
        for j in range(3):
            k = 3 * i + j
            g = [
                [grad[zo * 64 : zo * 64 + 64, j * 256 + p * 128 : j * 256 + p * 128 + 128] for p in range(2)]
                for zo in range(2)
            ]
            cb = pltpu.roll(g[0][0], 64, 1)
            ab = g[1][0] + jnp.where(is_low, g[0][1], cb)
            c_low = cb + pltpu.roll(g[1][1], 64, 1)
            t = 3 * k // 2
            if k % 2 == 0:
                column(t, ab)
                held_a = c_low
            else:
                ba = pltpu.roll(ab, 64, 1)
                column(t, jnp.where(is_low, held_a, ba))
                column(t + 1, jnp.where(is_low, ba, pltpu.roll(c_low, 64, 1)))
    column(13, jnp.where(is_low, held_a, 0.0))
    pl.semaphore_wait(barrier, len(greeted))
    first = send(sums.at[1 - core], half_in, other)

    slot_of, base_of = (0, 0, 1, 2), (0, 16, 0, 0)
    lane16 = lane_of((16, 128))

    def pack_sides(c, field, wide):
        for h in range(wide):
            for i in range(16):
                low, high = field[i, h : h + 1, :], field[i, 16 - wide + h : 17 - wide + h, :]
                y_out[0, 2 * c + h, i : i + 1, :] = low
                y_out[1, 2 * c + h, i : i + 1, :] = high
        packed = None
        for i in range(16):
            g = base_of[c] + i
            moved = pltpu.roll(field[i], 2 + 4 * g, 1)
            packed = moved if packed is None else jnp.where(lane16 // 4 == g, moved, packed)
        return packed

    sides_of = [pack_sides(c, vel.at[c], 2) for c in range(3)]
    z_out[0] = jnp.where(lane16 < 64, sides_of[0], sides_of[1])
    z_out[1] = sides_of[2]

    field = jnp.zeros((64, 128), F32)
    for half in range(2):
        for b in range(8):
            part = eddy_z[half, pl.ds(b, 64, stride=8), :]
            field = jnp.where(lane // 8 == 2 * b + half, part, field)
    field = 0.02 + field
    for i in range(8):
        for dx in range(2):
            for dy in range(2):
                ext[3, 2 + 2 * i + dx, pl.ds(8 + dy, 8, stride=2), :] = field[i * 8 : i * 8 + 8]
    z_out[2] = pack_sides(3, ext.at[3, 2:18, 8:24], 1)
    rims = [
        send(vel.at[:, 0:2], ext.at[0:3, 18:20, 8:24], x_down),
        send(vel.at[:, 14:16], ext.at[0:3, 0:2, 8:24], x_up),
        send(ext.at[3, 2:3, 8:24], ext.at[3, 18:19, 8:24], x_down),
        send(ext.at[3, 17:18, 8:24], ext.at[3, 1:2, 8:24], x_up),
        send(y_out.at[0], y_in.at[1], y_down),
        send(y_out.at[1], y_in.at[0], y_up),
        send(z_out, z_in, z_side),
    ]

    place_weights(w_hidden, None, back)
    widen(wide_del, jnp.concatenate([jnp.concatenate(d, axis=0) for d in deltas], axis=1))
    scatter = []
    first.wait_recv()
    half_sum[...] = sums[core] + half_in[...]
    for s, (dy, dx) in enumerate(steps):
        to, device = plane(dy, dx)
        scatter.append(
            send(half_sum.at[pl.ds(pl.multiple_of(to * 32, 32), 32)], chunk_in.at[s], device)
        )

    firsts, d_acts = [], []
    for half in range(2):
        d_act = None
        for i in range(3):
            term = dot(rows_of(wide_del, half, i), back[half, i])
            d_act = term if d_act is None else d_act + term
        d_acts.append(d_act)
    for half, d_act in enumerate(d_acts):
        d_first = (d_act * slope_one[:, half * 256 : half * 256 + 256]).astype(BF16).astype(F32)
        scaled = (d_first.reshape(64, 8, 256) * times.reshape(1, 8, 1)).reshape(512, 256)
        high = scaled.astype(BF16)
        low = (scaled - high.astype(F32)).astype(BF16)
        firsts.append((high.T, low.T))
    lhs = jnp.concatenate([firsts[0][0], firsts[1][0], firsts[0][1], firsts[1][1]], axis=0)
    packed = jnp.zeros((64, 128), F32)
    for i in range(3):
        grad = dot(lhs, first_in[i : i + 8].reshape(512, 128))
        grad = grad[:512] + grad[512:]
        summed = None
        for zo in range(8):
            part = grad[zo * 64 : zo * 64 + 64]
            shift = (-3 * (zo - 1)) % 128
            part = pltpu.roll(part, shift, 1) if shift else part
            summed = part if summed is None else summed + part
        for j in range(3):
            start = 9 * (3 * i + j)
            shift = (start - 32 * j) % 128
            moved = pltpu.roll(summed, shift, 1) if shift else summed
            packed = jnp.where((lane >= start) & (lane < start + 9), moved, packed)
    first_sums[...] = packed

    own32 = pl.ds(pl.multiple_of(core * 32, 32), 32)
    f_first = send(
        first_sums.at[pl.ds(pl.multiple_of((1 - core) * 32, 32), 32)], f_in, other
    )
    ext[0:3, 2:18, 8:24, :] = vel[...]
    f_first.wait_recv()
    mine = first_sums[own32, :] + f_in[...]
    f_sum[...] = mine
    f_plane[spot] = mine
    f_across = [send(f_sum, f_plane.at[spot], plane(dy, dx)[1]) for dy, dx in steps]

    for part in scatter:
        part.wait_recv()
    mine = half_sum[pl.ds(pl.multiple_of(spot * 32, 32), 32), :]
    for s in range(15):
        mine = mine + chunk_in[s]
    chunk_sum[...] = mine
    deep_in[depth] = mine
    deep = [send(chunk_sum, deep_in.at[depth], device) for device in deeper]

    for part in deep:
        part.wait_recv()
    mine = deep_in[0]
    for d in range(1, 8):
        mine = mine + deep_in[d]
    own = pl.ds(pl.multiple_of(spot * 32, 32), 32)
    total[core, own, :] = mine
    gather = [
        send(total.at[core, own], total.at[core, own], plane(dy, dx)[1]) for dy, dx in steps
    ]

    for part in f_across:
        part.wait_recv()
    mine = f_plane[0]
    for s in range(1, 16):
        mine = mine + f_plane[s]
    f_mid[...] = mine
    f_deep[depth] = mine
    f_planes = [send(f_mid, f_deep.at[depth], device) for device in deeper]

    for rim in rims:
        rim.wait_recv()
    for c in range(4):
        for h in range(1 if c == 3 else 2):
            for i in range(16):
                to = 7 if c == 3 else 6 + h
                ext[c, 2 + i, to : to + 1, :] = y_in[0, 2 * c + h, i : i + 1, :]
                ext[c, 2 + i, 24 + h : 25 + h, :] = y_in[1, 2 * c + h, i : i + 1, :]

    def row(i, carry):
        def beside(c, here, far):
            turn = (254 - 4 * (base_of[c] + i)) % 128
            edge = pltpu.roll(z_in[slot_of[c]], turn, 1)
            out = []
            for m in (1, 2) if far else (1,):
                after = jnp.where(lane16 < m, edge, here)
                before = jnp.where(lane16 >= 128 - m, edge, here)
                out += [pltpu.roll(after, 128 - m, 1), pltpu.roll(before, m, 1)]
            return out

        centre = ext[3, 2 + i, 8:24, :]
        sides = [
            (ext[3, 3 + i, 8:24, :], ext[3, 1 + i, 8:24, :]),
            (ext[3, 2 + i, 9:25, :], ext[3, 2 + i, 7:23, :]),
            beside(3, centre, False),
        ]
        sides = [(0.5 * (centre + a), 0.5 * (centre + b)) for a, b in sides]
        speed = [ext[c, 2 + i, 8:24, :] for c in range(3)]
        for c in range(3):
            here = speed[c]
            near = [
                [ext[c, 2 + i + m, 8:24, :] for m in (1, -1, 2, -2)],
                [ext[c, 2 + i, 8 + m : 24 + m, :] for m in (1, -1, 2, -2)],
                beside(c, here, True),
            ]
            change = None
            for axis in range(3):
                a1, b1, a2, b2 = near[axis]
                slope = (8.0 * (a1 - b1) - (a2 - b2)) * (1.0 / 12.0)
                term = sides[axis][0] * (a1 - here) - sides[axis][1] * (here - b1)
                term = term - speed[axis] * slope
                change = term if change is None else change + term
            u_next[c, i] = here + 0.2 * change
        return carry

    lax.fori_loop(0, 16, row, 0)
    hand_over(u_next, u_result)

    for part in f_planes:
        part.wait_recv()
    mine = f_deep[0]
    for d in range(1, 8):
        mine = mine + f_deep[d]
    f_total[own32, :] = mine
    f_last = send(f_total.at[own32], f_result.at[own32], other)
    hand_over(f_total.at[own32], f_result.at[own32])

    across = []
    for dy in range(4):
        for part, (sy, _) in zip(gather, steps):
            if sy == dy:
                part.wait_recv()
        rows = pl.ds(pl.multiple_of(((y + 4 - dy) % 4) * 128, 128), 128)
        across.append(send(total.at[core, rows], result.at[core, rows], other))
    hand_over(total.at[core], result.at[core])
    f_last.wait_recv()
    for part in across:
        part.wait_recv()
    for part in started:
        part.wait_send()
    for move in moves:
        move.wait()


SENDS = 7 + 1 + 15 + 1 + 15 + 7 + 7 + 15 + 1 + 4


def out_shapes():
    return (
        jax.ShapeDtypeStruct((3, 16, 16, 128), F32),
        jax.ShapeDtypeStruct((1, 1, 8), F32),
        jax.ShapeDtypeStruct((64, 81), F32),
        jax.ShapeDtypeStruct((64, 1728), F32),
        jax.ShapeDtypeStruct((1, 64), F32),
    )


def hand_out(
    u_source, f_source, source, u_result, loss_result, first_result, hidden_result, last_result,
    u_held, f_held, held, slot_loss, grad_first, grad_hidden, grad_last, sems,
):
    gx, gy, role = lax.axis_index("gx"), lax.axis_index("gy"), lax.axis_index("role")
    loads = [pltpu.make_async_copy(source.at[n], held.at[n], sems.at[n]) for n in range(2)]
    loads += [pltpu.make_async_copy(u_source.at[n], u_held.at[n], sems.at[2 + n]) for n in range(3)]
    loads.append(pltpu.make_async_copy(f_source, f_held, sems.at[5]))
    stores = [pltpu.make_async_copy(u_held.at[n], u_result.at[n], sems.at[6 + n]) for n in range(3)]
    stores += [
        pltpu.make_async_copy(grad_hidden, hidden_result, sems.at[9]),
        pltpu.make_async_copy(grad_first, first_result, sems.at[10]),
        pltpu.make_async_copy(grad_last, last_result, sems.at[11]),
        pltpu.make_async_copy(slot_loss, loss_result, sems.at[12]),
    ]
    for load in loads:
        load.start()
    for half in range(2):
        loads[half].wait()
        for t in range(7):
            start, width = half * 896 + t * 128, 64 if half == 1 and t == 6 else 128
            grad_hidden[:, start : start + width] = held[half, t * 64 : t * 64 + 64, :width]
    stores[3].start()
    for n in range(3):
        loads[2 + n].wait()
        stores[n].start()
    loads[5].wait()
    grad_first[...] = f_held[:, :81]
    grad_last[...] = held[1, 448:449, :64]
    losses = held[0, 448:464, :]
    at = lax.broadcasted_iota(jnp.int32, (16, 128), 0)
    losses = jnp.where(at == (gy * 2 + role) * 2 + gx // 16, losses, 0.0)
    losses = jnp.sum(losses, axis=0, keepdims=True)
    losses = pltpu.roll(losses, (128 - (gx % 16) * 8) % 128, 1)
    slot_loss[0] = losses[:, :8]
    for store in stores[4:]:
        store.start()
    for store in stores:
        store.wait()


def on_device(velocity, target_visc, w_first, w_hidden, w_last, sample_owner, sample_block):
    anywhere = pl.BlockSpec(memory_space=pl.ANY)
    spread = spread_matrix()
    rows = (pool_matrix(), target_matrix(), spread, spread[:8])
    consts = [jnp.asarray(np.concatenate(rows, 0)), jnp.asarray(first_selector())]
    args = [
        velocity, target_visc, w_first, w_hidden, w_last.reshape(1, 64),
        sample_owner.reshape(1, 256), sample_block.reshape(1, 256), *consts,
    ]
    sums = [
        jax.ShapeDtypeStruct(shape, F32) for shape in ((3, 16, 16, 128), (64, 128), (2, 512, 128))
    ]
    outs = pl.pallas_call(
        whole_kernel,
        out_shape=sums,
        in_specs=[anywhere] * 9,
        out_specs=(anywhere,) * 3,
        scratch_shapes=[pltpu.VMEM(a.shape, a.dtype) for a in args] + [
            pltpu.VMEM((3, 16, 16, 128), F32),
            pltpu.VMEM((512, 128), F32),
            pltpu.VMEM((10, 64, 128), BF16),
            pltpu.VMEM((3, 512, 128), BF16),
            pltpu.VMEM((2, 3, 256, 960), BF16),
            pltpu.VMEM((2, 3, 960, 256), BF16),
            pltpu.VMEM((2, 10, 64, 960), BF16),
            pltpu.VMEM((2, 10, 64, 960), BF16),
            pltpu.VMEM((512, 512), F32),
            pltpu.VMEM((4, 10, 64, 768), BF16),
            pltpu.VMEM((2, 512, 128), F32),
            pltpu.VMEM((2, 512, 128), F32),
            pltpu.VMEM((64, 128), F32),
            pltpu.VMEM((4, 20, 32, 128), F32),
            pltpu.VMEM((2, 7, 16, 128), F32),
            pltpu.VMEM((2, 7, 16, 128), F32),
            pltpu.VMEM((3, 16, 128), F32),
            pltpu.VMEM((3, 16, 128), F32),
            pltpu.VMEM((512, 128), F32),
            pltpu.VMEM((512, 128), F32),
            pltpu.VMEM((15, 32, 128), F32),
            pltpu.VMEM((32, 128), F32),
            pltpu.VMEM((8, 32, 128), F32),
            pltpu.VMEM((2, 512, 128), F32),
            pltpu.VMEM((32, 128), F32),
            pltpu.VMEM((32, 128), F32),
            pltpu.VMEM((16, 32, 128), F32),
            pltpu.VMEM((32, 128), F32),
            pltpu.VMEM((8, 32, 128), F32),
            pltpu.VMEM((64, 128), F32),
            pltpu.SemaphoreType.DMA((12,)),
            pltpu.SemaphoreType.DMA((2, SENDS)),
        ],
        compiler_params=pltpu.CompilerParams(
            vmem_limit_bytes=60 * 1024 * 1024, collective_id=0, has_side_effects=True
        ),
        name="whole",
    )(*args)
    outs = pl.pallas_call(
        hand_out,
        out_shape=out_shapes(),
        in_specs=[anywhere] * 3,
        out_specs=(anywhere,) * 5,
        scratch_shapes=[pltpu.VMEM(a.shape, a.dtype) for a in [*sums, *out_shapes()[1:]]]
        + [pltpu.SemaphoreType.DMA((13,))],
        compiler_params=pltpu.CompilerParams(vmem_limit_bytes=60 * 1024 * 1024),
        name="hand_out",
    )(*outs)
    u_next, slot_loss, grad_first, grad_hidden, grad_last = outs
    return (u_next, slot_loss, grad_first, grad_hidden, grad_last.reshape(64))


def solution(mesh):
    return jax.shard_map(
        on_device,
        mesh=mesh,
        in_specs=(
            P(None, "gx", "gy", "role"),
            P("gx", "gy", "role"),
            P(),
            P(),
            P(),
            P("gy", "role", None, None),
            P("gy", "role", None, None),
        ),
        out_specs=(P(None, "gx", "gy", "role"), P("gy", "role", "gx"), P(), P(), P()),
        check_vma=False,
    )
```
